256 devices in a mesh: tm: 16 (over z_lo, y, core), tile: 16 (over z_hi, x).
Axes of the slice: x: 4, y: 4, z: 8 (z_hi: 4, z_lo: 2; z = z_hi * 2 + z_lo), core: 2. Of those that a mesh axis runs over, the one named last changes fastest.
Arguments:
- queries: bfloat16 [65536, 4096], P(('tm', 'tile')), may hold values from -120 to 120
- keys: bfloat16 [65536, 4096], P(('tm', 'tile')), may hold values from -6 to 6
- values: bfloat16 [65536, 4096], P(('tm', 'tile')), may hold values from -6 to 6
- slot_tile: int32 [16, 16], replicated, may hold values from 0 to 15, each once within a row
- tile_mask: int32 [16, 16, 48], replicated, may hold values from 0 to 1, as said below
- token_count: int32 [16, 16], replicated, may hold values from 2 to 256
Outputs:
- attended: bfloat16 [65536, 4096], P(('tm', 'tile'))
The draws below stay inside these ranges and needn't reach their ends.
Inputs may be any that keep to these rules, and one draw needn't show every extreme that they name: Each row of slot_tile holds every spatial tile of 0 .. 15 once. `tile_mask`: every row has at most 11 ones, and exactly 11 in some row of every slab; entry [s, t, 16 + t] is always 1; candidates in slab -1 or slab 16 are 0.
All inputs are finite; a program needn't handle non-finite values.
Results may differ from the reference program's by a relative error of at most 0.0049.
Values may be sent and summed in bfloat16 or wider, within the bound.
A program may use at most 128 MiB of HBM per device.

```python
import jax
import jax.numpy as jnp
from jax import lax

HEADS = 32
HEAD_DIM = 128
KMAX = 11
TILE_TOK = 256
TILES = 16
SLABS = 16
TOKENS = 65536
WIDTH = 4096


def shared_keys(key):
    return jax.random.truncated_normal(jax.random.fold_in(key, 100), -6.0, 6.0, (TOKENS, WIDTH), jnp.float32)


def draw_keys(key, part):
    base = shared_keys(key)
    return base.astype(jnp.bfloat16)


def draw_queries(key, part):
    key = jax.random.fold_in(key, 21)
    normal_part = jax.random.fold_in(key, 0)
    drawn = jax.random.truncated_normal(normal_part, -6.0, 6.0, (TOKENS, WIDTH), jnp.float32)
    return drawn.astype(jnp.bfloat16)


def draw_tile_mask(key, part):
    key = jax.random.fold_in(key, 11)
    score_key, keep_key = jax.random.split(key)
    candidates = 3 * TILES
    raw_scores = jax.random.randint(score_key, (SLABS, TILES, candidates), 0, 2 ** 20)
    column = jnp.arange(candidates, dtype=jnp.int32)
    scores = raw_scores * candidates + column[None, None, :]
    slab_number = jnp.arange(SLABS, dtype=jnp.int32)[:, None, None]
    tile_number = jnp.arange(TILES, dtype=jnp.int32)[None, :, None]
    cand_block = column[None, None, :] // TILES
    cand_spatial = column[None, None, :] % TILES
    outside = (cand_block == 0) & (slab_number == 0) | (cand_block == 2) & (slab_number == SLABS - 1)
    centre = (cand_block == 1) & (cand_spatial == tile_number)
    scores = jnp.where(outside, -1, scores)
    scores = jnp.where(centre, 2 ** 30, scores)
    top_values, top_index = lax.top_k(scores, KMAX)
    keeping = jax.random.randint(keep_key, (SLABS, TILES, KMAX), 0, 4) > 0
    leading = (jnp.arange(KMAX, dtype=jnp.int32) == 0)[None, None, :]
    full_row = tile_number == 0
    keeping = (keeping | leading | full_row) & (top_values >= 0)
    hits = (top_index[:, :, :, None] == column[None, None, None, :]) & keeping[:, :, :, None]
    return jnp.any(hits, axis=2).astype(jnp.int32)


def draw_token_count(key, part):
    key = jax.random.fold_in(key, 12)
    ragged_key, full_key = jax.random.split(key)
    grid_shape = (SLABS, TILES)
    ragged = jax.random.randint(ragged_key, grid_shape, 2, TILE_TOK + 1)
    full_tiles = jax.random.randint(full_key, grid_shape, 0, 2) > 0
    tile_number = jnp.arange(TILES, dtype=jnp.int32)[None, :]
    slab_number = jnp.arange(SLABS, dtype=jnp.int32)[:, None]
    counts = jnp.where(full_tiles | (tile_number == 0), TILE_TOK, ragged)
    counts = jnp.where((tile_number == TILES - 1) & (slab_number == 0), 2, counts)
    return counts.astype(jnp.int32)


def block_levels(stream_key, shape, pieces, smallest, largest):
    loudness = 1.0
    for dim, shards_of in pieces:
        steps = jax.random.uniform(jax.random.fold_in(jax.random.fold_in(stream_key, 6), dim), (shards_of,), jnp.float32, smallest / len(pieces), largest / len(pieces))
        loudness = loudness * jnp.repeat(jnp.exp(steps), shape[dim] // shards_of).reshape((-1,) + (1,) * (len(shape) - 1 - dim))
    return loudness


def scatter_about(own_key, dims, deviation, bound, cuts=(), kind=jnp.bfloat16):
    loudness = block_levels(own_key, dims, cuts, -0.22, 0.18) if cuts else 1.0
    result = jax.random.normal(own_key, dims, jnp.float32) * deviation * loudness
    return jnp.minimum(jnp.maximum(result, -bound), bound).astype(kind)


def setup_inputs(seed: int = 0) -> dict:
    arg_keys = jax.random.split(jax.random.key(seed), 7)
    return {
        "queries": draw_queries(jax.random.fold_in(arg_keys[6], 71), 0),
        "keys": draw_keys(jax.random.fold_in(arg_keys[6], 71), 0),
        "values": scatter_about(arg_keys[2], (TOKENS, WIDTH), 1.0, 6.0, ((0, 256),)),
        "slot_tile": jax.vmap(lambda own: jax.random.permutation(own, TILES))(jax.random.split(arg_keys[3], SLABS)).reshape((SLABS, TILES)).astype(jnp.int32),
        "tile_mask": draw_tile_mask(jax.random.fold_in(arg_keys[6], 71), 0),
        "token_count": draw_token_count(jax.random.fold_in(arg_keys[6], 71), 0),
    }


def tile_plan(slab_index, slot_tile, tile_mask, token_count):
    slab_count = slot_tile.shape[0]
    tile_count = slot_tile.shape[1]
    tile_order = jnp.arange(tile_count, dtype=jnp.int32)
    near_slabs = jnp.clip(slab_index + jnp.arange(3, dtype=jnp.int32) - 1, 0, slab_count - 1).astype(jnp.int32)
    near_slots = slot_tile[near_slabs]
    inverse = jnp.sum(jnp.where(near_slots[:, :, None] == tile_order[None, None, :], tile_order[None, :, None], 0), axis=1).astype(jnp.int32)
    own_spatial = slot_tile[slab_index]
    mask_rows = tile_mask[slab_index][own_spatial]
    picked = jnp.argsort(1 - mask_rows, axis=1, stable=True)[:, :KMAX].astype(jnp.int32)
    picked_flags = jnp.take_along_axis(mask_rows, picked, axis=1)
    cand_block = (picked // tile_count).astype(jnp.int32)
    cand_spatial = (picked % tile_count).astype(jnp.int32)
    key_block = (cand_block * tile_count + inverse[cand_block, cand_spatial]).astype(jnp.int32)
    near_counts = token_count[near_slabs]
    key_counts = near_counts[cand_block, cand_spatial]
    position = jnp.arange(TILE_TOK, dtype=jnp.int32)
    key_live = (picked_flags[:, :, None] > 0) & (position[None, None, :] < key_counts[:, :, None])
    query_live = position[None, :] < token_count[slab_index][own_spatial][:, None]
    return key_block, key_live, query_live


def tile_attention(query_tile, key_tiles, value_tiles, key_live, query_live):
    score_scale = 1.0 / (HEAD_DIM ** 0.5)
    scores = jnp.einsum("qhd,kthd->hqkt", query_tile.astype(jnp.float32), key_tiles.astype(jnp.float32)) * score_scale
    scores = jnp.where(key_live[None, None, :, :], scores, -1e30)
    row_max = jnp.max(scores, axis=(2, 3), keepdims=True)
    exponent = jnp.exp(scores - row_max)
    denominator = jnp.sum(exponent, axis=(2, 3), keepdims=True)
    weights = lax.optimization_barrier((exponent / denominator).astype(jnp.bfloat16))
    outputs = jnp.einsum("hqkt,kthd->qhd", weights.astype(jnp.float32), value_tiles.astype(jnp.float32))
    outputs = jnp.where(query_live[:, None, None], outputs, 0.0)
    return outputs.astype(jnp.bfloat16)


def reference(queries, keys, values, slot_tile, tile_mask, token_count):
    grid_shape = (SLABS, TILES, TILE_TOK, HEADS, HEAD_DIM)
    query_grid = queries.reshape(grid_shape)
    empty_slab = jnp.zeros((1,) + grid_shape[1:], keys.dtype)
    key_padded = jnp.concatenate([empty_slab, keys.reshape(grid_shape), empty_slab], 0)
    value_padded = jnp.concatenate([empty_slab, values.reshape(grid_shape), empty_slab], 0)

    def per_slab(slab_index):
        key_block, key_live, query_live = tile_plan(slab_index, slot_tile, tile_mask, token_count)
        near_keys = lax.dynamic_slice_in_dim(key_padded, slab_index, 3, 0).reshape((3 * TILES,) + grid_shape[2:])
        near_values = lax.dynamic_slice_in_dim(value_padded, slab_index, 3, 0).reshape((3 * TILES,) + grid_shape[2:])
        slab_queries = query_grid[slab_index]

        def per_tile(tile_number):
            chosen = key_block[tile_number]
            return tile_attention(slab_queries[tile_number], near_keys[chosen], near_values[chosen], key_live[tile_number], query_live[tile_number])

        return lax.map(per_tile, jnp.arange(TILES, dtype=jnp.int32))

    attended = lax.map(per_slab, jnp.arange(SLABS, dtype=jnp.int32))
    return attended.reshape(TOKENS, WIDTH)
```

```python
import functools

import jax
import jax.numpy as jnp
from jax import lax
from jax.experimental import pallas as pl
from jax.experimental.pallas import tpu as pltpu
from jax.sharding import PartitionSpec as P

HEAD_DIM = 128
KMAX = 11
SIDE = 4
EXP2_SCALE = 1.4426950408889634 / HEAD_DIM**0.5
MESH = pl.DeviceIdType.MESH


def peer(slot, step):
    row = (slot // SIDE + step + 1) % SIDE
    column = (slot % SIDE + step // SIDE + 1) % SIDE
    return row * SIDE + column


def kernel(
    slabs,
    tiles,
    slot_ref,
    mask_ref,
    count_ref,
    q_hbm,
    k_hbm,
    v_hbm,
    out_hbm,
    k0,
    k1,
    v0,
    v1,
    q0,
    q1,
    o0,
    o1,
    live,
    scores,
    follow,
    block_of,
    send_sem,
    recv_sem,
    own_sem,
    pass_sem,
    near_sem,
    out_send,
    out_recv,
    out_own,
):
    slab = lax.axis_index("tm")
    slot = lax.axis_index("tile")
    tok = q_hbm.shape[0]
    keys, values, query, result = (k0, k1), (v0, v1), (q0, q1), (o0, o1)
    has_before = slab > 0
    has_after = slab < slabs - 1
    near_count = has_before.astype(jnp.int32) + has_after.astype(jnp.int32)

    barrier = pltpu.get_barrier_semaphore()

    def greet(step, carry):
        pl.semaphore_signal(barrier, inc=1, device_id={"tile": peer(slot, step)}, device_id_type=MESH)
        return carry

    lax.fori_loop(0, tiles - 1, greet, 0)

    @pl.when(has_before)
    def _():
        pl.semaphore_signal(barrier, inc=1, device_id={"tm": slab - 1}, device_id_type=MESH)

    @pl.when(has_after)
    def _():
        pl.semaphore_signal(barrier, inc=1, device_id={"tm": slab + 1}, device_id_type=MESH)

    pl.semaphore_wait(barrier, tiles - 1 + near_count)

    phases = (
        (k_hbm, k0, tiles, 0),
        (v_hbm, v0, tiles, 0),
        (k_hbm, k1, tiles, 1),
        (v_hbm, v1, tiles, 1),
        (q_hbm, q0, 0, 0),
        (q_hbm, q1, 0, 1),
    )

    def head_columns(owner, head):
        return pl.ds(pl.multiple_of((owner * 2 + head) * HEAD_DIM, HEAD_DIM), HEAD_DIM)

    def own_copy(phase):
        source, gathered, base, head = phases[phase]
        return pltpu.make_async_copy(
            source.at[:, head_columns(slot, head)], gathered.at[base + slot], own_sem.at[phase]
        )

    def spread(phase):
        source, gathered, base, head = phases[phase]
        own_copy(phase).start()

        def send(step, carry):
            other = peer(slot, step)
            pltpu.make_async_remote_copy(
                src_ref=source.at[:, head_columns(other, head)],
                dst_ref=gathered.at[base + slot],
                send_sem=send_sem.at[phase],
                recv_sem=recv_sem.at[phase],
                device_id={"tile": other},
                device_id_type=MESH,
            ).start()
            return carry

        lax.fori_loop(0, tiles - 1, send, 0)

    def arrive(phase):
        gathered, base = phases[phase][1], phases[phase][2]
        others = gathered.at[pl.ds(base, tiles - 1)]
        pltpu.make_async_copy(others, others, recv_sem.at[phase]).wait()
        own_copy(phase).wait()

    def passing(phase, way):
        gathered = phases[phase][1]
        return pltpu.make_async_remote_copy(
            src_ref=gathered.at[pl.ds(tiles, tiles)],
            dst_ref=gathered.at[pl.ds(0 if way > 0 else 2 * tiles, tiles)],
            send_sem=pass_sem.at[phase, (1 + way) // 2],
            recv_sem=near_sem.at[phase, (1 + way) // 2],
            device_id={"tm": slab + way},
            device_id_type=MESH,
        )

    def hand_on(phase):
        @pl.when(has_after)
        def _():
            passing(phase, 1).start()

        @pl.when(has_before)
        def _():
            passing(phase, -1).start()

    def near_arrive(phase):
        @pl.when(has_before)
        def _():
            passing(phase, 1).wait_recv()

        @pl.when(has_after)
        def _():
            passing(phase, -1).wait_recv()

    spread(0)
    spread(1)

    row = lax.broadcasted_iota(jnp.int32, (tok, HEAD_DIM), 0)
    for block in range(3):
        near = jnp.clip(slab + (block - 1), 0, slabs - 1)

        def place(index, carry, near=near, block=block):
            found = jnp.int32(0)
            for other in range(tiles):
                found = jnp.where(slot_ref[near, other] == index, other, found)
            block_of[block * tiles + index] = block * tiles + found
            count = count_ref[near, slot_ref[near, index]]
            live[block * tiles + index] = jnp.where(row < count, 1.0, 0.0).astype(jnp.bfloat16)
            return carry

        lax.fori_loop(0, tiles, place, 0)
    live[3 * tiles] = jnp.zeros((tok, HEAD_DIM), jnp.bfloat16)

    def chain(tile, carry):
        follow[tile, 3 * tiles] = 3 * tiles
        follow[tile, 3 * tiles + 1] = 3 * tiles

        def link(index, after):
            candidate = 3 * tiles - 1 - index
            first = jnp.where(mask_ref[slab, tile, candidate] > 0, candidate, after)
            follow[tile, candidate] = first
            return first

        lax.fori_loop(0, 3 * tiles, link, jnp.int32(3 * tiles))
        return carry

    lax.fori_loop(0, tiles, chain, 0)

    for phase in range(4):
        arrive(phase)
        hand_on(phase)
        spread(phase + 2)

    def out_copy(head, other):
        return pltpu.make_async_remote_copy(
            src_ref=result[head].at[other],
            dst_ref=out_hbm.at[:, head_columns(slot, head)],
            send_sem=out_send.at[head],
            recv_sem=out_recv.at[head],
            device_id={"tile": other},
            device_id_type=MESH,
        )

    def out_keep(head):
        return pltpu.make_async_copy(
            result[head].at[slot], out_hbm.at[:, head_columns(slot, head)], out_own.at[head]
        )

    def attend(head, at):
        tile = slot_ref[slab, at]
        own_block = block_of[tiles + tile]
        chosen = []
        candidate = follow[tile, 0]
        for _ in range(KMAX):
            listed = candidate < 3 * tiles
            spot = block_of[jnp.minimum(candidate, 3 * tiles - 1)]
            chosen.append((jnp.where(listed, spot, own_block), jnp.where(listed, spot, 3 * tiles)))
            candidate = follow[tile, candidate + 1]
        q_tile = query[head][at]
        best = jnp.full((tok, HEAD_DIM), -jnp.inf, jnp.float32)
        for number, (spot, _) in enumerate(chosen):
            k_tile = keys[head][spot]
            alive = live[spot]
            k_tile = k_tile * alive + k_tile[0:1] * (1 - alive)
            score = lax.dot_general(
                q_tile, k_tile, (((1,), (1,)), ((), ())), preferred_element_type=jnp.float32
            )
            scores[number] = score
            for part in range(tok // HEAD_DIM):
                best = jnp.maximum(best, score[:, part * HEAD_DIM : (part + 1) * HEAD_DIM])
        top = jnp.max(best, axis=1, keepdims=True) * EXP2_SCALE
        total = jnp.zeros((tok, 2 * HEAD_DIM), jnp.float32)
        for number, (spot, life) in enumerate(chosen):
            alive = live[life]
            weight = jnp.exp2(scores[number] * EXP2_SCALE - top).astype(jnp.bfloat16)
            v_tile = jnp.concatenate([values[head][spot] * alive, alive], axis=1)
            total = total + jnp.dot(weight, v_tile, preferred_element_type=jnp.float32)
        attended = total[:, :HEAD_DIM] / total[:, HEAD_DIM:]
        count = count_ref[slab, tile]
        result[head][at] = jnp.where(row < count, attended, 0.0).astype(jnp.bfloat16)

    for head in range(2):
        near_arrive(2 * head)
        near_arrive(2 * head + 1)
        arrive(4 + head)

        def turn(step, carry, head=head):
            at = peer(slot, step)
            attend(head, at)

            @pl.when(at != slot)
            def _():
                out_copy(head, at).start()

            @pl.when(at == slot)
            def _():
                out_keep(head).start()

            return carry

        lax.fori_loop(0, tiles, turn, 0)

    for head in range(2):
        blocks = out_hbm.at[:, pl.ds(0, (tiles - 1) * HEAD_DIM)]
        pltpu.make_async_copy(blocks, blocks, out_recv.at[head]).wait()
        out_keep(head).wait()
        sent = result[head].at[pl.ds(0, tiles - 1)]
        pltpu.make_async_copy(sent, sent, out_send.at[head]).wait()
    for phase in range(6):
        sent = q0.at[pl.ds(0, tiles - 1)]
        pltpu.make_async_copy(sent, sent, send_sem.at[phase]).wait()
    for phase in range(4):

        @pl.when(has_after)
        def _(phase=phase):
            passing(phase, 1).wait_send()

        @pl.when(has_before)
        def _(phase=phase):
            passing(phase, -1).wait_send()


def solution(mesh):
    slabs, tiles = mesh.shape["tm"], mesh.shape["tile"]

    def shards(queries, keys, values, slot_tile, tile_mask, token_count):
        tok, width = queries.shape
        near = pltpu.VMEM((3 * tiles, tok, HEAD_DIM), jnp.bfloat16)
        own = pltpu.VMEM((tiles, tok, HEAD_DIM), jnp.bfloat16)
        return pl.pallas_call(
            functools.partial(kernel, slabs, tiles),
            out_shape=jax.ShapeDtypeStruct((tok, width), jnp.bfloat16),
            in_specs=[pl.BlockSpec(memory_space=pltpu.SMEM)] * 3
            + [pl.BlockSpec(memory_space=pl.ANY)] * 3,
            out_specs=pl.BlockSpec(memory_space=pl.ANY),
            scratch_shapes=[near] * 4
            + [own] * 4
            + [
                pltpu.VMEM((3 * tiles + 1, tok, HEAD_DIM), jnp.bfloat16),
                pltpu.VMEM((KMAX, tok, tok), jnp.float32),
                pltpu.SMEM((tiles, 3 * tiles + 2), jnp.int32),
                pltpu.SMEM((3 * tiles,), jnp.int32),
                pltpu.SemaphoreType.DMA((6,)),
                pltpu.SemaphoreType.DMA((6,)),
                pltpu.SemaphoreType.DMA((6,)),
                pltpu.SemaphoreType.DMA((4, 2)),
                pltpu.SemaphoreType.DMA((4, 2)),
                pltpu.SemaphoreType.DMA((2,)),
                pltpu.SemaphoreType.DMA((2,)),
                pltpu.SemaphoreType.DMA((2,)),
            ],
            compiler_params=pltpu.CompilerParams(
                collective_id=0, has_side_effects=True, vmem_limit_bytes=48 * 1024 * 1024
            ),
        )(slot_tile, tile_mask, token_count, queries, keys, values)

    return jax.shard_map(
        shards,
        mesh=mesh,
        in_specs=(P(("tm", "tile"), None),) * 3 + (P(),) * 3,
        out_specs=P(("tm", "tile"), None),
        check_vma=False,
    )
```

```python
import functools

import jax
import jax.numpy as jnp
from jax import lax
from jax.experimental import pallas as pl
from jax.experimental.pallas import tpu as pltpu
from jax.sharding import PartitionSpec as P

HEAD_DIM = 128
KMAX = 11
SIDE = 4
AHEAD = 2
VMEM_BYTES = 60 * 1024 * 1024
EXP2_SCALE = 1.4426950408889634 / HEAD_DIM**0.5
MESH = pl.DeviceIdType.MESH


def peer(slot, step):
    row = (slot // SIDE + step + 1) % SIDE
    column = (slot % SIDE + step // SIDE + 1) % SIDE
    return row * SIDE + column


def origin(slot, step):
    row = (slot // SIDE + 5 * SIDE - 1 - step) % SIDE
    column = (slot % SIDE + 2 * SIDE - 1 - step // SIDE) % SIDE
    return row * SIDE + column


def kernel(
    slabs,
    tiles,
    slot_hbm,
    mask_hbm,
    count_hbm,
    q_hbm,
    k_hbm,
    v_hbm,
    out_hbm,
    k0,
    k1,
    v0,
    v1,
    q0,
    q1,
    o0,
    o1,
    live,
    score0,
    score1,
    top0,
    top1,
    k_raw,
    v_raw,
    fixed,
    relay,
    slot_ref,
    mask_ref,
    count_ref,
    follow,
    block_of,
    key_pick,
    value_pick,
    plan_sem,
    send_sem,
    recv_sem,
    query_sem,
    own_sem,
    pass_sem,
    near_sem,
    relay_send,
    relay_sem,
    out_send,
    out_recv,
    out_own,
):
    slab = lax.axis_index("tm")
    slot = lax.axis_index("tile")
    tok = q_hbm.shape[0]
    keys, values, query, result = (k0, k1), (v0, v1), (q0, q1), (o0, o1)
    has_before = slab > 0
    has_after = slab < slabs - 1
    near_count = has_before.astype(jnp.int32) + has_after.astype(jnp.int32)

    right = slabs // 2
    left = right - 1
    via_left = (left - 2, left - 4, left - 6)
    via_right = tuple(slabs - 1 - other for other in via_left)
    part = tiles // (len(via_left) + 1)
    at_meeting = (slab == left) | (slab == right)
    is_via = slab == via_left[0]
    for other in via_left[1:] + via_right:
        is_via = is_via | (slab == other)

    plan = [
        pltpu.make_async_copy(slot_hbm, slot_ref, plan_sem.at[0]),
        pltpu.make_async_copy(mask_hbm.at[slab], mask_ref, plan_sem.at[1]),
        pltpu.make_async_copy(count_hbm, count_ref, plan_sem.at[2]),
    ]
    raw = [
        pltpu.make_async_copy(k_hbm, k_raw, plan_sem.at[3]),
        pltpu.make_async_copy(v_hbm, v_raw, plan_sem.at[4]),
    ]
    for copy in plan + raw:
        copy.start()

    barrier = pltpu.get_barrier_semaphore()

    def greet_slab(other):
        pl.semaphore_signal(barrier, inc=1, device_id={"tm": other}, device_id_type=MESH)

    def greet(step, carry):
        pl.semaphore_signal(barrier, inc=1, device_id={"tile": peer(slot, step)}, device_id_type=MESH)
        return carry

    lax.fori_loop(0, tiles - 1, greet, 0)

    @pl.when(has_before)
    def _():
        greet_slab(slab - 1)

    @pl.when(has_after)
    def _():
        greet_slab(slab + 1)

    @pl.when(at_meeting)
    def _():
        for other in via_left + via_right:
            greet_slab(other)

    @pl.when(is_via)
    def _():
        greet_slab(left)
        greet_slab(right)

    extra = 6 * at_meeting.astype(jnp.int32) + 2 * is_via.astype(jnp.int32)
    pl.semaphore_wait(barrier, tiles - 1 + near_count + extra)

    for copy in plan + raw:
        copy.wait()
    row = lax.broadcasted_iota(jnp.int32, (tok, HEAD_DIM), 0)
    own_count = count_ref[slab, slot_ref[slab, slot]]
    own_alive = jnp.where(row < own_count, 1.0, 0.0).astype(jnp.bfloat16)

    phases = (
        (k_raw, k0, tiles, 0),
        (v_raw, v0, tiles, 0),
        (k_raw, k1, tiles, 1),
        (v_raw, v1, tiles, 1),
        (q_hbm, q0, 0, 0),
        (q_hbm, q1, 0, 1),
    )

    def head_columns(owner, head):
        return pl.ds(pl.multiple_of((owner * 2 + head) * HEAD_DIM, HEAD_DIM), HEAD_DIM)

    def own_query(head):
        return pltpu.make_async_copy(
            q_hbm.at[:, head_columns(slot, head)], query[head].at[slot], own_sem.at[head]
        )

    def spread(phase):
        source, gathered, base, head = phases[phase]
        if phase >= 4:
            own_query(head).start()

        def send(step, carry):
            other = peer(slot, step)
            if phase < 4:
                block = source[:, head_columns(other, head)]
                if phase % 2 == 0:
                    block = block * own_alive + block[0:1] * (1 - own_alive)
                else:
                    block = block * own_alive
                fixed[phase, other] = block
            pltpu.make_async_remote_copy(
                src_ref=fixed.at[phase, other] if phase < 4 else source.at[:, head_columns(other, head)],
                dst_ref=gathered.at[base + slot],
                send_sem=send_sem.at[phase],
                recv_sem=recv_sem.at[phase] if phase < 4 else query_sem.at[head, slot],
                device_id={"tile": other},
                device_id_type=MESH,
            ).start()
            return carry

        lax.fori_loop(0, tiles - 1, send, 0)
        if phase < 4:
            block = source[:, head_columns(slot, head)]
            if phase % 2 == 0:
                block = block * own_alive + block[0:1] * (1 - own_alive)
            else:
                block = block * own_alive
            gathered[base + slot] = block

    def arrive(phase):
        gathered, base = phases[phase][1], phases[phase][2]
        others = gathered.at[pl.ds(base, tiles - 1)]
        pltpu.make_async_copy(others, others, recv_sem.at[phase]).wait()

    def passing(phase, way, first=0, blocks=None):
        gathered = phases[phase][1]
        blocks = tiles if blocks is None else blocks
        return pltpu.make_async_remote_copy(
            src_ref=gathered.at[pl.ds(tiles + first, blocks)],
            dst_ref=gathered.at[pl.ds((0 if way > 0 else 2 * tiles) + first, blocks)],
            send_sem=pass_sem.at[phase, (1 + way) // 2],
            recv_sem=near_sem.at[phase, (1 + way) // 2],
            device_id={"tm": slab + way},
            device_id_type=MESH,
        )

    def to_relay(phase, index, other):
        return pltpu.make_async_remote_copy(
            src_ref=phases[phase][1].at[pl.ds(tiles + (index + 1) * part, part)],
            dst_ref=relay.at[phase],
            send_sem=relay_send.at[phase, index],
            recv_sem=relay_sem.at[phase],
            device_id={"tm": other},
            device_id_type=MESH,
        )

    def from_relay(phase, index, way):
        first = (0 if way > 0 else 2 * tiles) + (index + 1) * part
        return pltpu.make_async_remote_copy(
            src_ref=relay.at[phase],
            dst_ref=phases[phase][1].at[pl.ds(first, part)],
            send_sem=relay_send.at[phase, index],
            recv_sem=near_sem.at[phase, (1 + way) // 2],
            device_id={"tm": right if way > 0 else left},
            device_id_type=MESH,
        )

    def hand_on(phase):
        @pl.when(has_after & (slab != left))
        def _():
            passing(phase, 1).start()

        @pl.when(has_before & (slab != right))
        def _():
            passing(phase, -1).start()

        @pl.when(slab == left)
        def _():
            for index, other in enumerate(via_left):
                to_relay(phase, index, other).start()
            passing(phase, 1, 0, part).start()

        @pl.when(slab == right)
        def _():
            for index, other in enumerate(via_right):
                to_relay(phase, index, other).start()
            passing(phase, -1, 0, part).start()

    def relay_on(phase):
        for way, vias in ((1, via_left), (-1, via_right)):
            for index, other in enumerate(vias):

                @pl.when(slab == other)
                def _(way=way, index=index):
                    pltpu.make_async_copy(relay.at[phase], relay.at[phase], relay_sem.at[phase]).wait()
                    from_relay(phase, index, way).start()

    def near_arrive(phase):
        @pl.when(has_before)
        def _():
            passing(phase, 1).wait_recv()

        @pl.when(has_after)
        def _():
            passing(phase, -1).wait_recv()

    def handed_on(phase):
        @pl.when(has_after & (slab != left))
        def _():
            passing(phase, 1).wait_send()

        @pl.when(has_before & (slab != right))
        def _():
            passing(phase, -1).wait_send()

        for way, here, vias in ((1, left, via_left), (-1, right, via_right)):

            @pl.when(slab == here)
            def _(way=way, vias=vias):
                passing(phase, way, 0, part).wait_send()
                for index, other in enumerate(vias):
                    to_relay(phase, index, other).wait_send()

            for index, other in enumerate(vias):

                @pl.when(slab == other)
                def _(way=way, index=index):
                    from_relay(phase, index, way).wait_send()

    for phase in range(AHEAD):
        spread(phase)

    for block in range(3):
        near = jnp.clip(slab + (block - 1), 0, slabs - 1)

        def place(index, carry, near=near, block=block):
            found = jnp.int32(0)
            for other in range(tiles):
                found = jnp.where(slot_ref[near, other] == index, other, found)
            block_of[block * tiles + index] = block * tiles + found
            count = count_ref[near, slot_ref[near, index]]
            live[block * tiles + index] = jnp.where(row < count, 1.0, 0.0).astype(jnp.bfloat16)
            return carry

        lax.fori_loop(0, tiles, place, 0)
    nothing = jnp.zeros((tok, HEAD_DIM), jnp.bfloat16)
    live[3 * tiles] = nothing
    v0[3 * tiles] = nothing
    v1[3 * tiles] = nothing

    def chain(tile, carry):
        follow[tile, 3 * tiles] = 3 * tiles
        follow[tile, 3 * tiles + 1] = 3 * tiles

        def link(index, after):
            candidate = 3 * tiles - 1 - index
            first = jnp.where(mask_ref[tile, candidate] > 0, candidate, after)
            follow[tile, candidate] = first
            return first

        lax.fori_loop(0, 3 * tiles, link, jnp.int32(3 * tiles))
        return carry

    lax.fori_loop(0, tiles, chain, 0)

    def pick(at, carry):
        tile = slot_ref[slab, at]
        own_block = block_of[tiles + tile]
        candidate = follow[tile, 0]
        for number in range(KMAX):
            listed = candidate < 3 * tiles
            spot = block_of[jnp.minimum(candidate, 3 * tiles - 1)]
            key_pick[at, number] = jnp.where(listed, spot, own_block)
            value_pick[at, number] = jnp.where(listed, spot, 3 * tiles)
            candidate = follow[tile, candidate + 1]
        return carry

    lax.fori_loop(0, tiles, pick, 0)

    for phase in range(4):
        arrive(phase)
        hand_on(phase)
        if phase > 0:
            relay_on(phase - 1)
        if phase + AHEAD < len(phases):
            spread(phase + AHEAD)
    relay_on(3)

    def out_copy(head, other):
        return pltpu.make_async_remote_copy(
            src_ref=result[head].at[other],
            dst_ref=out_hbm.at[:, head_columns(slot, head)],
            send_sem=out_send.at[head],
            recv_sem=out_recv.at[head],
            device_id={"tile": other},
            device_id_type=MESH,
        )

    def out_keep(head):
        return pltpu.make_async_copy(
            result[head].at[slot], out_hbm.at[:, head_columns(slot, head)], out_own.at[head]
        )

    def work(head, ahead, ahead_scores, ahead_top, at=None, at_scores=None, at_top=None):
        q_tile = query[head][ahead]
        best = jnp.full((tok, HEAD_DIM), -jnp.inf, jnp.float32)
        if at is not None:
            top = jnp.concatenate([at_top[...]] * (tok // HEAD_DIM), axis=1)
            total = jnp.zeros((tok, 2 * HEAD_DIM), jnp.float32)
        for number in range(KMAX):
            score = lax.dot_general(
                q_tile,
                keys[head][key_pick[ahead, number]],
                (((1,), (1,)), ((), ())),
                preferred_element_type=jnp.float32,
            )
            ahead_scores[number] = score
            if at is not None:
                weight = jnp.exp2(at_scores[number] * EXP2_SCALE - top).astype(jnp.bfloat16)
                spot = value_pick[at, number]
                v_tile = jnp.concatenate([values[head][spot], live[spot]], axis=1)
                total = total + jnp.dot(weight, v_tile, preferred_element_type=jnp.float32)
            for start in range(0, tok, HEAD_DIM):
                best = jnp.maximum(best, score[:, start : start + HEAD_DIM])
        ahead_top[...] = jnp.broadcast_to(
            jnp.max(best, axis=1, keepdims=True) * EXP2_SCALE, (tok, HEAD_DIM)
        )
        if at is not None:
            attended = total[:, :HEAD_DIM] / total[:, HEAD_DIM:]
            count = count_ref[slab, slot_ref[slab, at]]
            result[head][at] = jnp.where(row < count, attended, 0.0).astype(jnp.bfloat16)

    def query_arrive(head, step):
        at = origin(slot, step)

        @pl.when(step < tiles - 1)
        def _():
            block = query[head].at[at]
            pltpu.make_async_copy(block, block, query_sem.at[head, at]).wait()

        @pl.when(step == tiles - 1)
        def _():
            own_query(head).wait()

    for head in range(2):
        near_arrive(2 * head)
        near_arrive(2 * head + 1)
        query_arrive(head, 0)
        work(head, origin(slot, 0), score0, top0)

        def turn(pair, carry, head=head):
            even = 2 * pair
            query_arrive(head, even + 1)
            work(head, origin(slot, even + 1), score1, top1, origin(slot, even), score0, top0)
            out_copy(head, origin(slot, even)).start()

            @pl.when(even + 2 < tiles)
            def _():
                query_arrive(head, even + 2)

            later = jnp.minimum(even + 2, tiles - 1)
            work(head, origin(slot, later), score0, top0, origin(slot, even + 1), score1, top1)

            @pl.when(even + 2 < tiles)
            def _():
                out_copy(head, origin(slot, even + 1)).start()

            @pl.when(even + 2 == tiles)
            def _():
                out_keep(head).start()

            return carry

        lax.fori_loop(0, tiles // 2, turn, 0)

    for head in range(2):
        blocks = out_hbm.at[:, pl.ds(0, (tiles - 1) * HEAD_DIM)]
        pltpu.make_async_copy(blocks, blocks, out_recv.at[head]).wait()
        out_keep(head).wait()
        gone = result[head].at[pl.ds(0, tiles - 1)]
        pltpu.make_async_copy(gone, gone, out_send.at[head]).wait()
    for phase in range(6):
        gone = q0.at[pl.ds(0, tiles - 1)]
        pltpu.make_async_copy(gone, gone, send_sem.at[phase]).wait()
    for phase in range(4):
        handed_on(phase)


def solution(mesh):
    slabs, tiles = mesh.shape["tm"], mesh.shape["tile"]

    def shards(queries, keys, values, slot_tile, tile_mask, token_count):
        tok, width = queries.shape
        near = pltpu.VMEM((3 * tiles, tok, HEAD_DIM), jnp.bfloat16)
        near_zero = pltpu.VMEM((3 * tiles + 1, tok, HEAD_DIM), jnp.bfloat16)
        own = pltpu.VMEM((tiles, tok, HEAD_DIM), jnp.bfloat16)
        return pl.pallas_call(
            functools.partial(kernel, slabs, tiles),
            out_shape=jax.ShapeDtypeStruct((tok, width), jnp.bfloat16),
            in_specs=[pl.BlockSpec(memory_space=pl.ANY)] * 6,
            out_specs=pl.BlockSpec(memory_space=pl.ANY),
            scratch_shapes=[near, near, near_zero, near_zero]
            + [own] * 4
            + [
                near_zero,
                pltpu.VMEM((KMAX, tok, tok), jnp.float32),
                pltpu.VMEM((KMAX, tok, tok), jnp.float32),
                pltpu.VMEM((tok, HEAD_DIM), jnp.float32),
                pltpu.VMEM((tok, HEAD_DIM), jnp.float32),
                pltpu.VMEM((tok, width), jnp.bfloat16),
                pltpu.VMEM((tok, width), jnp.bfloat16),
                pltpu.VMEM((4, tiles, tok, HEAD_DIM), jnp.bfloat16),
                pltpu.VMEM((4, tiles // 4, tok, HEAD_DIM), jnp.bfloat16),
                pltpu.SMEM(slot_tile.shape, jnp.int32),
                pltpu.SMEM(tile_mask.shape[1:], jnp.int32),
                pltpu.SMEM(token_count.shape, jnp.int32),
                pltpu.SMEM((tiles, 3 * tiles + 2), jnp.int32),
                pltpu.SMEM((3 * tiles,), jnp.int32),
                pltpu.SMEM((tiles, KMAX), jnp.int32),
                pltpu.SMEM((tiles, KMAX), jnp.int32),
                pltpu.SemaphoreType.DMA((5,)),
                pltpu.SemaphoreType.DMA((6,)),
                pltpu.SemaphoreType.DMA((4,)),
                pltpu.SemaphoreType.DMA((2, tiles)),
                pltpu.SemaphoreType.DMA((2,)),
                pltpu.SemaphoreType.DMA((4, 2)),
                pltpu.SemaphoreType.DMA((4, 2)),
                pltpu.SemaphoreType.DMA((4, 3)),
                pltpu.SemaphoreType.DMA((4,)),
                pltpu.SemaphoreType.DMA((2,)),
                pltpu.SemaphoreType.DMA((2,)),
                pltpu.SemaphoreType.DMA((2,)),
            ],
            compiler_params=pltpu.CompilerParams(
                collective_id=0, has_side_effects=True, vmem_limit_bytes=VMEM_BYTES
            ),
        )(slot_tile, tile_mask, token_count, queries, keys, values)

    return jax.shard_map(
        shards,
        mesh=mesh,
        in_specs=(P(("tm", "tile"), None),) * 3 + (P(),) * 3,
        out_specs=P(("tm", "tile"), None),
        check_vma=False,
    )
```

```python
import functools

import jax
import jax.numpy as jnp
from jax import lax
from jax.experimental import pallas as pl
from jax.experimental.pallas import tpu as pltpu
from jax.sharding import PartitionSpec as P

HEAD_DIM = 128
KMAX = 11
SIDE = 4
RING = 8
OWNERS = SIDE * RING
VMEM_BYTES = 60 * 1024 * 1024
EXP2_SCALE = 1.4426950408889634 / HEAD_DIM**0.5
MESH = pl.DeviceIdType.MESH


def kernel(
    slabs,
    tiles,
    slot_hbm,
    mask_hbm,
    count_hbm,
    q_hbm,
    k_hbm,
    v_hbm,
    out_hbm,
    keys,
    values,
    query,
    result,
    live,
    score0,
    score1,
    top0,
    top1,
    k_raw,
    v_raw,
    k_fixed,
    v_fixed,
    slot_ref,
    mask_ref,
    count_ref,
    follow,
    block_of,
    key_pick,
    value_pick,
    plan_sem,
    send_sem,
    recv_sem,
    query_sem,
    own_sem,
    pass_sem,
    near_sem,
    out_send,
    out_recv,
    out_own,
):
    half_slabs = slabs // 2
    near = 3 * tiles
    slab = lax.axis_index("tm")
    slot = lax.axis_index("tile")
    half, place = slab // half_slabs, slab % half_slabs
    z, x = 2 * (slot // SIDE) + half, slot % SIDE
    tok = q_hbm.shape[0]

    def device(other_z, other_x):
        other_slab = (other_z % 2) * half_slabs + place
        return {"tm": other_slab, "tile": (other_z // 2) * SIDE + other_x}

    def partner(step):
        return (z + step + 1) % RING, (x + step // RING + 1) % SIDE

    def origin(step):
        return (z + 5 * RING - 1 - step) % RING, (x + 2 * SIDE - 1 - step // RING) % SIDE

    def block_at(other_z, other_x):
        return (other_z % 2) * tiles + (other_z // 2) * SIDE + other_x

    def head_columns(other_z, other_x):
        return pl.ds(pl.multiple_of((other_z * SIDE + other_x) * HEAD_DIM, HEAD_DIM), HEAD_DIM)

    first = [
        pltpu.make_async_copy(slot_hbm, slot_ref, plan_sem.at[0]),
        pltpu.make_async_copy(mask_hbm.at[place], mask_ref.at[0], plan_sem.at[1]),
        pltpu.make_async_copy(mask_hbm.at[place + half_slabs], mask_ref.at[1], plan_sem.at[2]),
        pltpu.make_async_copy(count_hbm, count_ref, plan_sem.at[3]),
        pltpu.make_async_copy(k_hbm, k_raw, plan_sem.at[4]),
        pltpu.make_async_copy(v_hbm, v_raw, plan_sem.at[5]),
    ]
    for copy in first:
        copy.start()

    def beside(way):
        return {"tm": half * half_slabs + (place + half_slabs + way) % half_slabs}

    barrier = pltpu.get_barrier_semaphore()

    def greet(step, carry):
        pl.semaphore_signal(
            barrier, inc=1, device_id=device(*partner(step)), device_id_type=MESH
        )
        return carry

    lax.fori_loop(0, OWNERS - 1, greet, 0)
    for way in (1, -1):
        pl.semaphore_signal(barrier, inc=1, device_id=beside(way), device_id_type=MESH)
    pl.semaphore_wait(barrier, OWNERS + 1)

    for copy in first:
        copy.wait()
    row = lax.broadcasted_iota(jnp.int32, (tok, HEAD_DIM), 0)
    own_count = count_ref[slab, slot_ref[slab, slot]]
    own_alive = jnp.where(row < own_count, 1.0, 0.0).astype(jnp.bfloat16)
    own_block = half * near + tiles + slot

    def k_block(columns):
        block = k_raw[:, columns]
        return block * own_alive + block[0:1] * (1 - own_alive)

    def v_block(columns):
        return v_raw[:, columns] * own_alive

    def own_query():
        return pltpu.make_async_copy(
            q_hbm.at[:, head_columns(z, x)], query.at[block_at(z, x)], own_sem.at[0]
        )

    spans = ((0, OWNERS // 2), (OWNERS // 2, OWNERS - 1))

    def spread(part):
        kind = part // 2
        start, stop = spans[part % 2]

        def send(step, carry):
            other = partner(step)
            columns = head_columns(*other)
            if kind == 0:
                k_fixed[step] = k_block(columns)
                source, target, arrived = k_fixed.at[step], keys.at[own_block], recv_sem.at[part]
            elif kind == 1:
                v_fixed[step] = v_block(columns)
                source, target, arrived = v_fixed.at[step], values.at[own_block], recv_sem.at[part]
            else:
                source, target = q_hbm.at[:, columns], query.at[block_at(z, x)]
                arrived = query_sem.at[block_at(z, x)]
            pltpu.make_async_remote_copy(
                src_ref=source,
                dst_ref=target,
                send_sem=send_sem.at[part],
                recv_sem=arrived,
                device_id=device(*other),
                device_id_type=MESH,
            ).start()
            return carry

        lax.fori_loop(start, stop, send, 0)
        if part == 1:
            keys[own_block] = k_block(head_columns(z, x))
        elif part == 3:
            values[own_block] = v_block(head_columns(z, x))
        elif part == 5:
            own_query().start()

    def arrive(part):
        start, stop = spans[part % 2]
        blocks = (keys, values)[part // 2].at[pl.ds(0, stop - start)]
        pltpu.make_async_copy(blocks, blocks, recv_sem.at[part]).wait()

    def passing(kind, way, which):
        gathered = (keys, values)[kind]
        turned = place == (half_slabs - 1 if way > 0 else 0)
        target = which + way * turned.astype(jnp.int32)
        exists = (target >= 0) & (target < 2)
        target = jnp.clip(target, 0, 1)
        copy = pltpu.make_async_remote_copy(
            src_ref=gathered.at[pl.ds(which * near + tiles, tiles)],
            dst_ref=gathered.at[pl.ds(target * near + (0 if way > 0 else 2 * tiles), tiles)],
            send_sem=pass_sem.at[kind, (1 + way) // 2, which],
            recv_sem=near_sem.at[kind, (1 + way) // 2, target],
            device_id=beside(way),
            device_id_type=MESH,
        )
        return exists, copy

    def hand_on(kind):
        for way in (1, -1):
            for which in range(2):
                exists, copy = passing(kind, way, which)
                pl.when(exists)(copy.start)

    def handed_on(kind):
        for way in (1, -1):
            for which in range(2):
                exists, copy = passing(kind, way, which)
                pl.when(exists)(copy.wait_send)

    def near_arrive(kind):
        for way in (1, -1):
            for which in range(2):
                before = place + half_slabs * which - way
                blocks = (keys, values)[kind].at[pl.ds(0, tiles)]
                copy = pltpu.make_async_copy(
                    blocks, blocks, near_sem.at[kind, (1 + way) // 2, which]
                )
                pl.when((before >= 0) & (before < slabs))(copy.wait)

    spread(0)
    spread(1)

    nothing = jnp.zeros((tok, HEAD_DIM), jnp.bfloat16)
    live[2 * near] = nothing
    values[2 * near] = nothing
    for which in range(2):
        for block in range(3):
            there = jnp.clip(place + half_slabs * which + (block - 1), 0, slabs - 1)
            base = which * near + block * tiles

            def seat(index, carry, there=there, base=base):
                found = jnp.int32(0)
                for other in range(tiles):
                    found = jnp.where(slot_ref[there, other] == index, other, found)
                block_of[base + index] = base + found
                count = count_ref[there, slot_ref[there, index]]
                live[base + index] = jnp.where(row < count, 1.0, 0.0).astype(jnp.bfloat16)
                return carry

            lax.fori_loop(0, tiles, seat, 0)

        def chain(tile, carry, which=which):
            at = which * tiles + tile
            follow[at, near] = near
            follow[at, near + 1] = near

            def link(index, after):
                candidate = near - 1 - index
                listed = jnp.where(mask_ref[which, tile, candidate] > 0, candidate, after)
                follow[at, candidate] = listed
                return listed

            lax.fori_loop(0, near, link, jnp.int32(near))
            return carry

        lax.fori_loop(0, tiles, chain, 0)

        def pick(at, carry, which=which):
            tile = slot_ref[place + half_slabs * which, at]
            centre = block_of[which * near + tiles + tile]
            candidate = follow[which * tiles + tile, 0]
            for number in range(KMAX):
                listed = candidate < near
                spot = block_of[which * near + jnp.minimum(candidate, near - 1)]
                key_pick[which * tiles + at, number] = jnp.where(listed, spot, centre)
                value_pick[which * tiles + at, number] = jnp.where(listed, spot, 2 * near)
                candidate = follow[which * tiles + tile, candidate + 1]
            return carry

        lax.fori_loop(0, tiles, pick, 0)

    for part in range(4):
        arrive(part)
        if part % 2 == 1:
            hand_on(part // 2)
        spread(part + 2)

    def out_copy(step):
        other = origin(step)
        return pltpu.make_async_remote_copy(
            src_ref=result.at[block_at(*other)],
            dst_ref=out_hbm.at[:, head_columns(z, x)],
            send_sem=out_send.at[0],
            recv_sem=out_recv.at[0],
            device_id=device(*other),
            device_id_type=MESH,
        )

    def out_keep():
        return pltpu.make_async_copy(
            result.at[block_at(z, x)], out_hbm.at[:, head_columns(z, x)], out_own.at[0]
        )

    def work(ahead, ahead_scores, ahead_top, at=None, at_scores=None, at_top=None):
        q_tile = query[ahead]
        best = jnp.full((tok, HEAD_DIM), -jnp.inf, jnp.float32)
        if at is not None:
            top = jnp.concatenate([at_top[...]] * (tok // HEAD_DIM), axis=1)
            total = jnp.zeros((tok, 2 * HEAD_DIM), jnp.float32)
        for number in range(KMAX):
            score = lax.dot_general(
                q_tile,
                keys[key_pick[ahead, number]],
                (((1,), (1,)), ((), ())),
                preferred_element_type=jnp.float32,
            )
            ahead_scores[number] = score
            if at is not None:
                weight = jnp.exp2(at_scores[number] * EXP2_SCALE - top).astype(jnp.bfloat16)
                spot = value_pick[at, number]
                v_tile = jnp.concatenate([values[spot], live[spot]], axis=1)
                total = total + jnp.dot(weight, v_tile, preferred_element_type=jnp.float32)
            for start in range(0, tok, HEAD_DIM):
                best = jnp.maximum(best, score[:, start : start + HEAD_DIM])
        ahead_top[...] = jnp.broadcast_to(
            jnp.max(best, axis=1, keepdims=True) * EXP2_SCALE, (tok, HEAD_DIM)
        )
        if at is not None:
            attended = total[:, :HEAD_DIM] / total[:, HEAD_DIM:]
            at_half, at_slot = at // tiles, at % tiles
            at_slab = place + half_slabs * at_half
            count = count_ref[at_slab, slot_ref[at_slab, at_slot]]
            result[at] = jnp.where(row < count, attended, 0.0).astype(jnp.bfloat16)

    def query_arrive(step):
        at = block_at(*origin(step))

        @pl.when(step < OWNERS - 1)
        def _():
            block = query.at[at]
            pltpu.make_async_copy(block, block, query_sem.at[at]).wait()

        @pl.when(step == OWNERS - 1)
        def _():
            own_query().wait()

    near_arrive(0)
    near_arrive(1)
    query_arrive(0)
    work(block_at(*origin(0)), score0, top0)

    def turn(pair, carry):
        even = 2 * pair
        at, after = block_at(*origin(even)), block_at(*origin(even + 1))
        query_arrive(even + 1)
        work(after, score1, top1, at, score0, top0)
        out_copy(even).start()

        @pl.when(even + 2 < OWNERS)
        def _():
            query_arrive(even + 2)

        later = block_at(*origin(jnp.minimum(even + 2, OWNERS - 1)))
        work(later, score0, top0, after, score1, top1)

        @pl.when(even + 2 < OWNERS)
        def _():
            out_copy(even + 1).start()

        @pl.when(even + 2 == OWNERS)
        def _():
            out_keep().start()

        return carry

    lax.fori_loop(0, OWNERS // 2, turn, 0)

    blocks = out_hbm.at[:, pl.ds(0, (OWNERS - 1) * HEAD_DIM)]
    pltpu.make_async_copy(blocks, blocks, out_recv.at[0]).wait()
    out_keep().wait()
    gone = result.at[pl.ds(0, OWNERS - 1)]
    pltpu.make_async_copy(gone, gone, out_send.at[0]).wait()
    for part in range(6):
        start, stop = spans[part % 2]
        gone = query.at[pl.ds(0, stop - start)]
        pltpu.make_async_copy(gone, gone, send_sem.at[part]).wait()
    handed_on(0)
    handed_on(1)


def solution(mesh):
    slabs, tiles = mesh.shape["tm"], mesh.shape["tile"]

    def shards(queries, keys, values, slot_tile, tile_mask, token_count):
        tok, width = queries.shape
        near = 3 * tiles

        def blocks(number):
            return pltpu.VMEM((number, tok, HEAD_DIM), jnp.bfloat16)

        return pl.pallas_call(
            functools.partial(kernel, slabs, tiles),
            out_shape=jax.ShapeDtypeStruct((tok, width), jnp.bfloat16),
            in_specs=[pl.BlockSpec(memory_space=pl.ANY)] * 6,
            out_specs=pl.BlockSpec(memory_space=pl.ANY),
            scratch_shapes=[
                blocks(2 * near),
                blocks(2 * near + 1),
                blocks(2 * tiles),
                blocks(2 * tiles),
                blocks(2 * near + 1),
                pltpu.VMEM((KMAX, tok, tok), jnp.float32),
                pltpu.VMEM((KMAX, tok, tok), jnp.float32),
                pltpu.VMEM((tok, HEAD_DIM), jnp.float32),
                pltpu.VMEM((tok, HEAD_DIM), jnp.float32),
                pltpu.VMEM((tok, width), jnp.bfloat16),
                pltpu.VMEM((tok, width), jnp.bfloat16),
                blocks(OWNERS),
                blocks(OWNERS),
                pltpu.SMEM(slot_tile.shape, jnp.int32),
                pltpu.SMEM((2,) + tile_mask.shape[1:], jnp.int32),
                pltpu.SMEM(token_count.shape, jnp.int32),
                pltpu.SMEM((2 * tiles, near + 2), jnp.int32),
                pltpu.SMEM((2 * near,), jnp.int32),
                pltpu.SMEM((2 * tiles, KMAX), jnp.int32),
                pltpu.SMEM((2 * tiles, KMAX), jnp.int32),
                pltpu.SemaphoreType.DMA((6,)),
                pltpu.SemaphoreType.DMA((6,)),
                pltpu.SemaphoreType.DMA((4,)),
                pltpu.SemaphoreType.DMA((2 * tiles,)),
                pltpu.SemaphoreType.DMA((1,)),
                pltpu.SemaphoreType.DMA((2, 2, 2)),
                pltpu.SemaphoreType.DMA((2, 2, 2)),
                pltpu.SemaphoreType.DMA((1,)),
                pltpu.SemaphoreType.DMA((1,)),
                pltpu.SemaphoreType.DMA((1,)),
            ],
            compiler_params=pltpu.CompilerParams(
                collective_id=0, has_side_effects=True, vmem_limit_bytes=VMEM_BYTES
            ),
        )(slot_tile, tile_mask, token_count, queries, keys, values)

    return jax.shard_map(
        shards,
        mesh=mesh,
        in_specs=(P(("tm", "tile"), None),) * 3 + (P(),) * 3,
        out_specs=P(("tm", "tile"), None),
        check_vma=False,
    )
```

```python
import functools

import jax
import jax.numpy as jnp
from jax import lax
from jax.experimental import pallas as pl
from jax.experimental.pallas import tpu as pltpu
from jax.sharding import PartitionSpec as P

HEAD_DIM = 128
KMAX = 11
SIDE = 4
RING = 8
OWNERS = SIDE * RING
SETTLE_PARTS = 4
VMEM_BYTES = 56 * 1024 * 1024
EXP2_SCALE = 1.4426950408889634 / HEAD_DIM**0.5
MESH = pl.DeviceIdType.MESH


def kernel(
    slabs,
    tiles,
    slot_hbm,
    mask_hbm,
    count_hbm,
    q_hbm,
    k_hbm,
    v_hbm,
    out_hbm,
    keys,
    values,
    query,
    result,
    live,
    score0,
    score1,
    top0,
    top1,
    k_raw,
    v_raw,
    k_fixed,
    v_fixed,
    slot_ref,
    mask_ref,
    count_ref,
    follow,
    block_of,
    key_pick,
    value_pick,
    plan_sem,
    send_sem,
    recv_sem,
    query_sem,
    own_sem,
    pass_sem,
    near_sem,
    out_send,
    out_recv,
    out_own,
):
    half_slabs = slabs // 2
    near = 3 * tiles
    slab = lax.axis_index("tm")
    slot = lax.axis_index("tile")
    half, place = slab // half_slabs, slab % half_slabs
    z, x = 2 * (slot // SIDE) + half, slot % SIDE
    tok = q_hbm.shape[0]

    def device(other_z, other_x):
        other_slab = (other_z % 2) * half_slabs + place
        return {"tm": other_slab, "tile": (other_z // 2) * SIDE + other_x}

    def partner(step):
        return (z + step + 1) % RING, (x + step // RING + 1) % SIDE

    def origin(step):
        return (z + 5 * RING - 1 - step) % RING, (x + 2 * SIDE - 1 - step // RING) % SIDE

    def block_at(other_z, other_x):
        return (other_z % 2) * tiles + (other_z // 2) * SIDE + other_x

    def head_columns(other_z, other_x):
        return pl.ds(pl.multiple_of((other_z * SIDE + other_x) * HEAD_DIM, HEAD_DIM), HEAD_DIM)

    upper, lower = pl.ds(0, tok // 2), pl.ds(tok // 2, tok // 2)
    first = [
        pltpu.make_async_copy(slot_hbm, slot_ref, plan_sem.at[0]),
        pltpu.make_async_copy(count_hbm, count_ref, plan_sem.at[1]),
        pltpu.make_async_copy(k_hbm.at[upper], k_raw.at[upper], plan_sem.at[2]),
        pltpu.make_async_copy(k_hbm.at[lower], k_raw.at[lower], plan_sem.at[3]),
        pltpu.make_async_copy(v_hbm, v_raw, plan_sem.at[4]),
        pltpu.make_async_copy(mask_hbm.at[place], mask_ref.at[0], plan_sem.at[5]),
        pltpu.make_async_copy(mask_hbm.at[place + half_slabs], mask_ref.at[1], plan_sem.at[6]),
    ]
    def beside(way):
        return {"tm": half * half_slabs + (place + half_slabs + way) % half_slabs}

    barrier = pltpu.get_barrier_semaphore()

    def greet(step, carry):
        pl.semaphore_signal(
            barrier, inc=1, device_id=device(*partner(step)), device_id_type=MESH
        )
        return carry

    lax.fori_loop(0, OWNERS - 1, greet, 0)
    for way in (1, -1):
        pl.semaphore_signal(barrier, inc=1, device_id=beside(way), device_id_type=MESH)
    for copy in first:
        copy.start()
    pl.semaphore_wait(barrier, OWNERS + 1)

    for copy in first[:4]:
        copy.wait()
    row = lax.broadcasted_iota(jnp.int32, (tok, HEAD_DIM), 0)
    own_count = count_ref[slab, slot_ref[slab, slot]]
    own_alive = jnp.where(row < own_count, 1.0, 0.0).astype(jnp.bfloat16)
    own_block = half * near + tiles + slot

    def k_block(columns):
        block = k_raw[:, columns]
        return block * own_alive + block[0:1] * (1 - own_alive)

    def v_block(columns):
        return v_raw[:, columns] * own_alive

    def own_query():
        return pltpu.make_async_copy(
            q_hbm.at[:, head_columns(z, x)], query.at[block_at(z, x)], own_sem.at[0]
        )

    spans = ((0, OWNERS // 2), (OWNERS // 2, OWNERS - 1))

    def spread(part):
        kind = part // 2
        start, stop = spans[part % 2]

        def send(step, carry):
            other = partner(step)
            columns = head_columns(*other)
            if kind == 0:
                k_fixed[step] = k_block(columns)
                source, target, arrived = k_fixed.at[step], keys.at[own_block], recv_sem.at[part]
            elif kind == 1:
                v_fixed[step] = v_block(columns)
                source, target, arrived = v_fixed.at[step], values.at[own_block], recv_sem.at[part]
            else:
                source, target = q_hbm.at[:, columns], query.at[block_at(z, x)]
                arrived = query_sem.at[block_at(z, x)]
            pltpu.make_async_remote_copy(
                src_ref=source,
                dst_ref=target,
                send_sem=send_sem.at[part],
                recv_sem=arrived,
                device_id=device(*other),
                device_id_type=MESH,
            ).start()
            return carry

        lax.fori_loop(start, stop, send, 0)
        if part == 1:
            keys[own_block] = k_block(head_columns(z, x))
        elif part == 3:
            values[own_block] = v_block(head_columns(z, x))
        elif part == 5:
            own_query().start()

    def arrive(part):
        start, stop = spans[part % 2]
        blocks = (keys, values)[part // 2].at[pl.ds(0, stop - start)]
        pltpu.make_async_copy(blocks, blocks, recv_sem.at[part]).wait()

    def passing(kind, way, which):
        gathered = (keys, values)[kind]
        turned = place == (half_slabs - 1 if way > 0 else 0)
        target = which + way * turned.astype(jnp.int32)
        exists = (target >= 0) & (target < 2)
        target = jnp.clip(target, 0, 1)
        copy = pltpu.make_async_remote_copy(
            src_ref=gathered.at[pl.ds(which * near + tiles, tiles)],
            dst_ref=gathered.at[pl.ds(target * near + (0 if way > 0 else 2 * tiles), tiles)],
            send_sem=pass_sem.at[kind, (1 + way) // 2, which],
            recv_sem=near_sem.at[kind, (1 + way) // 2, target],
            device_id=beside(way),
            device_id_type=MESH,
        )
        return exists, copy

    def hand_on(kind):
        for way in (1, -1):
            for which in range(2):
                exists, copy = passing(kind, way, which)
                pl.when(exists)(copy.start)

    def handed_on(kind):
        for way in (1, -1):
            for which in range(2):
                exists, copy = passing(kind, way, which)
                pl.when(exists)(copy.wait_send)

    def near_arrive(kind):
        for way in (1, -1):
            for which in range(2):
                before = place + half_slabs * which - way
                blocks = (keys, values)[kind].at[pl.ds(0, tiles)]
                copy = pltpu.make_async_copy(
                    blocks, blocks, near_sem.at[kind, (1 + way) // 2, which]
                )
                pl.when((before >= 0) & (before < slabs))(copy.wait)

    spread(0)
    spread(1)
    for copy in first[4:]:
        copy.wait()

    nothing = jnp.zeros((tok, HEAD_DIM), jnp.bfloat16)
    live[2 * near] = nothing
    values[2 * near] = nothing
    for which in range(2):
        for block in range(3):
            there = jnp.clip(place + half_slabs * which + (block - 1), 0, slabs - 1)
            base = which * near + block * tiles

            def seat(index, carry, there=there, base=base):
                found = jnp.int32(0)
                for other in range(tiles):
                    found = jnp.where(slot_ref[there, other] == index, other, found)
                block_of[base + index] = base + found
                count = count_ref[there, slot_ref[there, index]]
                live[base + index] = jnp.where(row < count, 1.0, 0.0).astype(jnp.bfloat16)
                return carry

            lax.fori_loop(0, tiles, seat, 0)

        def chain(tile, carry, which=which):
            at = which * tiles + tile
            follow[at, near] = near
            follow[at, near + 1] = near

            def link(index, after):
                candidate = near - 1 - index
                listed = jnp.where(mask_ref[which, tile, candidate] > 0, candidate, after)
                follow[at, candidate] = listed
                return listed

            lax.fori_loop(0, near, link, jnp.int32(near))
            return carry

        lax.fori_loop(0, tiles, chain, 0)

        def pick(at, carry, which=which):
            tile = slot_ref[place + half_slabs * which, at]
            centre = block_of[which * near + tiles + tile]
            candidate = follow[which * tiles + tile, 0]
            for number in range(KMAX):
                listed = candidate < near
                spot = block_of[which * near + jnp.minimum(candidate, near - 1)]
                key_pick[which * tiles + at, number] = jnp.where(listed, spot, centre)
                value_pick[which * tiles + at, number] = jnp.where(listed, spot, 2 * near)
                candidate = follow[which * tiles + tile, candidate + 1]
            return carry

        lax.fori_loop(0, tiles, pick, 0)

    for part in range(4):
        arrive(part)
        if part % 2 == 1:
            hand_on(part // 2)
        spread(part + 2)

    def out_copy(step):
        other = origin(step)
        return pltpu.make_async_remote_copy(
            src_ref=result.at[block_at(*other)],
            dst_ref=out_hbm.at[:, head_columns(z, x)],
            send_sem=out_send.at[0],
            recv_sem=out_recv.at[0],
            device_id=device(*other),
            device_id_type=MESH,
        )

    def out_keep():
        return pltpu.make_async_copy(
            result.at[block_at(z, x)], out_hbm.at[:, head_columns(z, x)], out_own.at[0]
        )

    def work(ahead, ahead_scores, ahead_top, at=None, at_scores=None, at_top=None):
        q_tile = query[ahead]
        best = jnp.full((tok, HEAD_DIM), -jnp.inf, jnp.float32)
        if at is not None:
            top = jnp.concatenate([at_top[...]] * (tok // HEAD_DIM), axis=1)
            total = jnp.zeros((tok, 2 * HEAD_DIM), jnp.float32)
        for number in range(KMAX):
            score = lax.dot_general(
                q_tile,
                keys[key_pick[ahead, number]],
                (((1,), (1,)), ((), ())),
                preferred_element_type=jnp.float32,
            )
            ahead_scores[number] = score
            if at is not None:
                weight = jnp.exp2(at_scores[number] * EXP2_SCALE - top).astype(jnp.bfloat16)
                spot = value_pick[at, number]
                v_tile = jnp.concatenate([values[spot], live[spot]], axis=1)
                total = total + jnp.dot(weight, v_tile, preferred_element_type=jnp.float32)
            for start in range(0, tok, HEAD_DIM):
                best = jnp.maximum(best, score[:, start : start + HEAD_DIM])
        ahead_top[...] = jnp.broadcast_to(
            jnp.max(best, axis=1, keepdims=True) * EXP2_SCALE, (tok, HEAD_DIM)
        )
        if at is not None:
            attended = total[:, :HEAD_DIM] / total[:, HEAD_DIM:]
            at_half, at_slot = at // tiles, at % tiles
            at_slab = place + half_slabs * at_half
            count = count_ref[at_slab, slot_ref[at_slab, at_slot]]
            result[at] = jnp.where(row < count, attended, 0.0).astype(jnp.bfloat16)

    def query_arrive(step):
        at = block_at(*origin(step))

        @pl.when(step < OWNERS - 1)
        def _():
            block = query.at[at]
            pltpu.make_async_copy(block, block, query_sem.at[at]).wait()

        @pl.when(step == OWNERS - 1)
        def _():
            own_query().wait()

    near_arrive(0)
    near_arrive(1)
    query_arrive(0)
    work(block_at(*origin(0)), score0, top0)

    def turn(pair, carry):
        even = 2 * pair
        at, after = block_at(*origin(even)), block_at(*origin(even + 1))
        query_arrive(even + 1)
        work(after, score1, top1, at, score0, top0)
        out_copy(even).start()

        @pl.when(even + 2 < OWNERS)
        def _():
            query_arrive(even + 2)

        later = block_at(*origin(jnp.minimum(even + 2, OWNERS - 1)))
        work(later, score0, top0, after, score1, top1)

        @pl.when(even + 2 < OWNERS)
        def _():
            out_copy(even + 1).start()

        @pl.when(even + 2 == OWNERS)
        def _():
            out_keep().start()

        return carry

    lax.fori_loop(0, OWNERS // 2, turn, 0)

    blocks = out_hbm.at[:, pl.ds(0, (OWNERS - 1) * HEAD_DIM)]
    pltpu.make_async_copy(blocks, blocks, out_recv.at[0]).wait()
    out_keep().wait()
    gone = result.at[pl.ds(0, OWNERS - 1)]
    pltpu.make_async_copy(gone, gone, out_send.at[0]).wait()
    for part in range(6):
        start, stop = spans[part % 2]
        gone = query.at[pl.ds(0, stop - start)]
        pltpu.make_async_copy(gone, gone, send_sem.at[part]).wait()
    handed_on(0)
    handed_on(1)


def settle(source, target, held, sems):
    rows = source.shape[0] // SETTLE_PARTS
    spans = [pl.ds(part * rows, rows) for part in range(SETTLE_PARTS)]
    come = [pltpu.make_async_copy(source.at[s], held.at[s], sems.at[0, i]) for i, s in enumerate(spans)]
    go = [pltpu.make_async_copy(held.at[s], target.at[s], sems.at[1, i]) for i, s in enumerate(spans)]
    for copy in come:
        copy.start()
    for before, after in zip(come, go):
        before.wait()
        after.start()
    for copy in go:
        copy.wait()


def solution(mesh):
    slabs, tiles = mesh.shape["tm"], mesh.shape["tile"]

    def shards(queries, keys, values, slot_tile, tile_mask, token_count):
        tok, width = queries.shape
        near = 3 * tiles

        def blocks(number):
            return pltpu.VMEM((number, tok, HEAD_DIM), jnp.bfloat16)

        attended = pl.pallas_call(
            functools.partial(kernel, slabs, tiles),
            out_shape=jax.ShapeDtypeStruct((tok, width), jnp.bfloat16),
            in_specs=[pl.BlockSpec(memory_space=pl.ANY)] * 6,
            out_specs=pl.BlockSpec(memory_space=pl.ANY),
            scratch_shapes=[
                blocks(2 * near),
                blocks(2 * near + 1),
                blocks(2 * tiles),
                blocks(2 * tiles),
                blocks(2 * near + 1),
                pltpu.VMEM((KMAX, tok, tok), jnp.float32),
                pltpu.VMEM((KMAX, tok, tok), jnp.float32),
                pltpu.VMEM((tok, HEAD_DIM), jnp.float32),
                pltpu.VMEM((tok, HEAD_DIM), jnp.float32),
                pltpu.VMEM((tok, width), jnp.bfloat16),
                pltpu.VMEM((tok, width), jnp.bfloat16),
                blocks(OWNERS),
                blocks(OWNERS),
                pltpu.SMEM(slot_tile.shape, jnp.int32),
                pltpu.SMEM((2,) + tile_mask.shape[1:], jnp.int32),
                pltpu.SMEM(token_count.shape, jnp.int32),
                pltpu.SMEM((2 * tiles, near + 2), jnp.int32),
                pltpu.SMEM((2 * near,), jnp.int32),
                pltpu.SMEM((2 * tiles, KMAX), jnp.int32),
                pltpu.SMEM((2 * tiles, KMAX), jnp.int32),
                pltpu.SemaphoreType.DMA((7,)),
                pltpu.SemaphoreType.DMA((6,)),
                pltpu.SemaphoreType.DMA((4,)),
                pltpu.SemaphoreType.DMA((2 * tiles,)),
                pltpu.SemaphoreType.DMA((1,)),
                pltpu.SemaphoreType.DMA((2, 2, 2)),
                pltpu.SemaphoreType.DMA((2, 2, 2)),
                pltpu.SemaphoreType.DMA((1,)),
                pltpu.SemaphoreType.DMA((1,)),
                pltpu.SemaphoreType.DMA((1,)),
            ],
            compiler_params=pltpu.CompilerParams(
                collective_id=0, has_side_effects=True, vmem_limit_bytes=VMEM_BYTES
            ),
        )(slot_tile, tile_mask, token_count, queries, keys, values)
        return pl.pallas_call(
            settle,
            out_shape=jax.ShapeDtypeStruct((tok, width), jnp.bfloat16),
            in_specs=[pl.BlockSpec(memory_space=pl.ANY)],
            out_specs=pl.BlockSpec(memory_space=pl.ANY),
            scratch_shapes=[
                pltpu.VMEM((tok, width), jnp.bfloat16),
                pltpu.SemaphoreType.DMA((2, SETTLE_PARTS)),
            ],
            compiler_params=pltpu.CompilerParams(vmem_limit_bytes=VMEM_BYTES),
        )(attended)

    return jax.shard_map(
        shards,
        mesh=mesh,
        in_specs=(P(("tm", "tile"), None),) * 3 + (P(),) * 3,
        out_specs=P(("tm", "tile"), None),
        check_vma=False,
    )
```

```python
import functools

import jax
import jax.numpy as jnp
from jax import lax
from jax.experimental import pallas as pl
from jax.experimental.pallas import tpu as pltpu
from jax.sharding import PartitionSpec as P

HEAD_DIM = 128
KMAX = 11
SIDE = 4
RING = 8
OWNERS = SIDE * RING
SETTLE_PARTS = 4
VMEM_BYTES = 56 * 1024 * 1024
EXP2_SCALE = 1.4426950408889634 / HEAD_DIM**0.5
MESH = pl.DeviceIdType.MESH


def kernel(
    slabs,
    tiles,
    slot_hbm,
    mask_hbm,
    count_hbm,
    q_hbm,
    k_hbm,
    v_hbm,
    out_hbm,
    keys,
    values,
    query,
    result,
    live,
    score0,
    score1,
    top0,
    top1,
    k_raw,
    v_raw,
    k_fixed,
    v_fixed,
    slot_ref,
    mask_ref,
    count_ref,
    follow,
    block_of,
    key_pick,
    value_pick,
    plan_sem,
    send_sem,
    recv_sem,
    query_sem,
    own_sem,
    pass_sem,
    near_sem,
    out_send,
    out_recv,
    out_own,
):
    half_slabs = slabs // 2
    near = 3 * tiles
    slab = lax.axis_index("tm")
    slot = lax.axis_index("tile")
    half, place = slab // half_slabs, slab % half_slabs
    z, x = 2 * (slot // SIDE) + half, slot % SIDE
    tok = q_hbm.shape[0]

    def device(other_z, other_x):
        other_slab = (other_z % 2) * half_slabs + place
        return {"tm": other_slab, "tile": (other_z // 2) * SIDE + other_x}

    def partner(step):
        return (z + step + 1) % RING, (x + step // RING + 1) % SIDE

    def origin(step):
        return (z + 5 * RING - 1 - step) % RING, (x + 2 * SIDE - 1 - step // RING) % SIDE

    def block_at(other_z, other_x):
        return (other_z % 2) * tiles + (other_z // 2) * SIDE + other_x

    def head_columns(other_z, other_x):
        return pl.ds(pl.multiple_of((other_z * SIDE + other_x) * HEAD_DIM, HEAD_DIM), HEAD_DIM)

    upper, lower = pl.ds(0, tok // 2), pl.ds(tok // 2, tok // 2)
    first = [
        pltpu.make_async_copy(slot_hbm, slot_ref, plan_sem.at[0]),
        pltpu.make_async_copy(count_hbm, count_ref, plan_sem.at[1]),
        pltpu.make_async_copy(k_hbm.at[upper], k_raw.at[upper], plan_sem.at[2]),
        pltpu.make_async_copy(k_hbm.at[lower], k_raw.at[lower], plan_sem.at[3]),
        pltpu.make_async_copy(v_hbm, v_raw, plan_sem.at[4]),
        pltpu.make_async_copy(mask_hbm.at[place], mask_ref.at[0], plan_sem.at[5]),
        pltpu.make_async_copy(mask_hbm.at[place + half_slabs], mask_ref.at[1], plan_sem.at[6]),
    ]
    def beside(way):
        return {"tm": half * half_slabs + (place + half_slabs + way) % half_slabs}

    barrier = pltpu.get_barrier_semaphore()
    for reach in (4, 3, 5, 2, 6, 1, 7, 0):
        for shift in range(SIDE):
            if reach or shift:
                other = (z + reach) % RING, (x + shift) % SIDE
                pl.semaphore_signal(
                    barrier, inc=1, device_id=device(*other), device_id_type=MESH
                )
    for way in (1, -1):
        pl.semaphore_signal(barrier, inc=1, device_id=beside(way), device_id_type=MESH)
    for copy in first:
        copy.start()
    pl.semaphore_wait(barrier, OWNERS + 1)

    for copy in first[:4]:
        copy.wait()
    row = lax.broadcasted_iota(jnp.int32, (tok, HEAD_DIM), 0)
    own_count = count_ref[slab, slot_ref[slab, slot]]
    own_alive = jnp.where(row < own_count, 1.0, 0.0).astype(jnp.bfloat16)
    own_block = half * near + tiles + slot

    def k_block(columns):
        block = k_raw[:, columns]
        return block * own_alive + block[0:1] * (1 - own_alive)

    def v_block(columns):
        return v_raw[:, columns] * own_alive

    def own_query():
        return pltpu.make_async_copy(
            q_hbm.at[:, head_columns(z, x)], query.at[block_at(z, x)], own_sem.at[0]
        )

    spans = ((0, OWNERS // 2), (OWNERS // 2, OWNERS - 1))

    def spread(part):
        kind = part // 2
        start, stop = spans[part % 2]

        def send(step, carry):
            other = partner(step)
            columns = head_columns(*other)
            if kind == 0:
                k_fixed[step] = k_block(columns)
                source, target, arrived = k_fixed.at[step], keys.at[own_block], recv_sem.at[part]
            elif kind == 1:
                v_fixed[step] = v_block(columns)
                source, target, arrived = v_fixed.at[step], values.at[own_block], recv_sem.at[part]
            else:
                source, target = q_hbm.at[:, columns], query.at[block_at(z, x)]
                arrived = query_sem.at[block_at(z, x)]
            pltpu.make_async_remote_copy(
                src_ref=source,
                dst_ref=target,
                send_sem=send_sem.at[part],
                recv_sem=arrived,
                device_id=device(*other),
                device_id_type=MESH,
            ).start()
            return carry

        lax.fori_loop(start, stop, send, 0)
        if part == 1:
            keys[own_block] = k_block(head_columns(z, x))
        elif part == 3:
            values[own_block] = v_block(head_columns(z, x))
        elif part == 5:
            own_query().start()

    def arrive(part):
        start, stop = spans[part % 2]
        blocks = (keys, values)[part // 2].at[pl.ds(0, stop - start)]
        pltpu.make_async_copy(blocks, blocks, recv_sem.at[part]).wait()

    def passing(kind, way, which):
        gathered = (keys, values)[kind]
        turned = place == (half_slabs - 1 if way > 0 else 0)
        target = which + way * turned.astype(jnp.int32)
        exists = (target >= 0) & (target < 2)
        target = jnp.clip(target, 0, 1)
        copy = pltpu.make_async_remote_copy(
            src_ref=gathered.at[pl.ds(which * near + tiles, tiles)],
            dst_ref=gathered.at[pl.ds(target * near + (0 if way > 0 else 2 * tiles), tiles)],
            send_sem=pass_sem.at[kind, (1 + way) // 2, which],
            recv_sem=near_sem.at[kind, (1 + way) // 2, target],
            device_id=beside(way),
            device_id_type=MESH,
        )
        return exists, copy

    def hand_on(kind):
        for way in (1, -1):
            for which in range(2):
                exists, copy = passing(kind, way, which)
                pl.when(exists)(copy.start)

    def handed_on(kind):
        for way in (1, -1):
            for which in range(2):
                exists, copy = passing(kind, way, which)
                pl.when(exists)(copy.wait_send)

    def near_arrive(kind):
        for way in (1, -1):
            for which in range(2):
                before = place + half_slabs * which - way
                blocks = (keys, values)[kind].at[pl.ds(0, tiles)]
                copy = pltpu.make_async_copy(
                    blocks, blocks, near_sem.at[kind, (1 + way) // 2, which]
                )
                pl.when((before >= 0) & (before < slabs))(copy.wait)

    spread(0)
    spread(1)
    for copy in first[4:]:
        copy.wait()

    nothing = jnp.zeros((tok, HEAD_DIM), jnp.bfloat16)
    live[2 * near] = nothing
    values[2 * near] = nothing
    for which in range(2):
        for block in range(3):
            there = jnp.clip(place + half_slabs * which + (block - 1), 0, slabs - 1)
            base = which * near + block * tiles

            def seat(index, carry, there=there, base=base):
                found = jnp.int32(0)
                for other in range(tiles):
                    found = jnp.where(slot_ref[there, other] == index, other, found)
                block_of[base + index] = base + found
                count = count_ref[there, slot_ref[there, index]]
                live[base + index] = jnp.where(row < count, 1.0, 0.0).astype(jnp.bfloat16)
                return carry

            lax.fori_loop(0, tiles, seat, 0)

        def chain(tile, carry, which=which):
            at = which * tiles + tile
            follow[at, near] = near
            follow[at, near + 1] = near

            def link(index, after):
                candidate = near - 1 - index
                listed = jnp.where(mask_ref[which, tile, candidate] > 0, candidate, after)
                follow[at, candidate] = listed
                return listed

            lax.fori_loop(0, near, link, jnp.int32(near))
            return carry

        lax.fori_loop(0, tiles, chain, 0)

        def pick(at, carry, which=which):
            tile = slot_ref[place + half_slabs * which, at]
            centre = block_of[which * near + tiles + tile]
            candidate = follow[which * tiles + tile, 0]
            for number in range(KMAX):
                listed = candidate < near
                spot = block_of[which * near + jnp.minimum(candidate, near - 1)]
                key_pick[which * tiles + at, number] = jnp.where(listed, spot, centre)
                value_pick[which * tiles + at, number] = jnp.where(listed, spot, 2 * near)
                candidate = follow[which * tiles + tile, candidate + 1]
            return carry

        lax.fori_loop(0, tiles, pick, 0)

    for part in range(4):
        arrive(part)
        if part % 2 == 1:
            hand_on(part // 2)
        spread(part + 2)

    def out_copy(step):
        other = origin(step)
        return pltpu.make_async_remote_copy(
            src_ref=result.at[block_at(*other)],
            dst_ref=out_hbm.at[:, head_columns(z, x)],
            send_sem=out_send.at[0],
            recv_sem=out_recv.at[0],
            device_id=device(*other),
            device_id_type=MESH,
        )

    def out_keep():
        return pltpu.make_async_copy(
            result.at[block_at(z, x)], out_hbm.at[:, head_columns(z, x)], out_own.at[0]
        )

    def work(ahead, ahead_scores, ahead_top, at=None, at_scores=None, at_top=None):
        q_tile = query[ahead]
        best = jnp.full((tok, HEAD_DIM), -jnp.inf, jnp.float32)
        if at is not None:
            top = jnp.concatenate([at_top[...]] * (tok // HEAD_DIM), axis=1)
            total = jnp.zeros((tok, 2 * HEAD_DIM), jnp.float32)
        for number in range(KMAX):
            score = lax.dot_general(
                q_tile,
                keys[key_pick[ahead, number]],
                (((1,), (1,)), ((), ())),
                preferred_element_type=jnp.float32,
            )
            ahead_scores[number] = score
            if at is not None:
                weight = jnp.exp2(at_scores[number] * EXP2_SCALE - top).astype(jnp.bfloat16)
                spot = value_pick[at, number]
                v_tile = jnp.concatenate([values[spot], live[spot]], axis=1)
                total = total + jnp.dot(weight, v_tile, preferred_element_type=jnp.float32)
            for start in range(0, tok, HEAD_DIM):
                best = jnp.maximum(best, score[:, start : start + HEAD_DIM])
        ahead_top[...] = jnp.broadcast_to(
            jnp.max(best, axis=1, keepdims=True) * EXP2_SCALE, (tok, HEAD_DIM)
        )
        if at is not None:
            attended = total[:, :HEAD_DIM] / total[:, HEAD_DIM:]
            at_half, at_slot = at // tiles, at % tiles
            at_slab = place + half_slabs * at_half
            count = count_ref[at_slab, slot_ref[at_slab, at_slot]]
            result[at] = jnp.where(row < count, attended, 0.0).astype(jnp.bfloat16)

    def query_arrive(step):
        at = block_at(*origin(step))

        @pl.when(step < OWNERS - 1)
        def _():
            block = query.at[at]
            pltpu.make_async_copy(block, block, query_sem.at[at]).wait()

        @pl.when(step == OWNERS - 1)
        def _():
            own_query().wait()

    near_arrive(0)
    near_arrive(1)
    query_arrive(0)
    work(block_at(*origin(0)), score0, top0)

    def turn(pair, carry):
        even = 2 * pair
        at, after = block_at(*origin(even)), block_at(*origin(even + 1))
        query_arrive(even + 1)
        work(after, score1, top1, at, score0, top0)
        out_copy(even).start()

        @pl.when(even + 2 < OWNERS)
        def _():
            query_arrive(even + 2)

        later = block_at(*origin(jnp.minimum(even + 2, OWNERS - 1)))
        work(later, score0, top0, after, score1, top1)

        @pl.when(even + 2 < OWNERS)
        def _():
            out_copy(even + 1).start()

        @pl.when(even + 2 == OWNERS)
        def _():
            out_keep().start()

        return carry

    lax.fori_loop(0, OWNERS // 2, turn, 0)

    blocks = out_hbm.at[:, pl.ds(0, (OWNERS - 1) * HEAD_DIM)]
    pltpu.make_async_copy(blocks, blocks, out_recv.at[0]).wait()
    out_keep().wait()
    gone = result.at[pl.ds(0, OWNERS - 1)]
    pltpu.make_async_copy(gone, gone, out_send.at[0]).wait()
    for part in range(6):
        start, stop = spans[part % 2]
        gone = query.at[pl.ds(0, stop - start)]
        pltpu.make_async_copy(gone, gone, send_sem.at[part]).wait()
    handed_on(0)
    handed_on(1)


def settle(source, target, held, sems):
    rows = source.shape[0] // SETTLE_PARTS
    spans = [pl.ds(part * rows, rows) for part in range(SETTLE_PARTS)]
    come = [pltpu.make_async_copy(source.at[s], held.at[s], sems.at[0, i]) for i, s in enumerate(spans)]
    go = [pltpu.make_async_copy(held.at[s], target.at[s], sems.at[1, i]) for i, s in enumerate(spans)]
    for copy in come:
        copy.start()
    for before, after in zip(come, go):
        before.wait()
        after.start()
    for copy in go:
        copy.wait()


def solution(mesh):
    slabs, tiles = mesh.shape["tm"], mesh.shape["tile"]

    def shards(queries, keys, values, slot_tile, tile_mask, token_count):
        tok, width = queries.shape
        near = 3 * tiles

        def blocks(number):
            return pltpu.VMEM((number, tok, HEAD_DIM), jnp.bfloat16)

        attended = pl.pallas_call(
            functools.partial(kernel, slabs, tiles),
            out_shape=jax.ShapeDtypeStruct((tok, width), jnp.bfloat16),
            in_specs=[pl.BlockSpec(memory_space=pl.ANY)] * 6,
            out_specs=pl.BlockSpec(memory_space=pl.ANY),
            scratch_shapes=[
                blocks(2 * near),
                blocks(2 * near + 1),
                blocks(2 * tiles),
                blocks(2 * tiles),
                blocks(2 * near + 1),
                pltpu.VMEM((KMAX, tok, tok), jnp.float32),
                pltpu.VMEM((KMAX, tok, tok), jnp.float32),
                pltpu.VMEM((tok, HEAD_DIM), jnp.float32),
                pltpu.VMEM((tok, HEAD_DIM), jnp.float32),
                pltpu.VMEM((tok, width), jnp.bfloat16),
                pltpu.VMEM((tok, width), jnp.bfloat16),
                blocks(OWNERS),
                blocks(OWNERS),
                pltpu.SMEM(slot_tile.shape, jnp.int32),
                pltpu.SMEM((2,) + tile_mask.shape[1:], jnp.int32),
                pltpu.SMEM(token_count.shape, jnp.int32),
                pltpu.SMEM((2 * tiles, near + 2), jnp.int32),
                pltpu.SMEM((2 * near,), jnp.int32),
                pltpu.SMEM((2 * tiles, KMAX), jnp.int32),
                pltpu.SMEM((2 * tiles, KMAX), jnp.int32),
                pltpu.SemaphoreType.DMA((7,)),
                pltpu.SemaphoreType.DMA((6,)),
                pltpu.SemaphoreType.DMA((4,)),
                pltpu.SemaphoreType.DMA((2 * tiles,)),
                pltpu.SemaphoreType.DMA((1,)),
                pltpu.SemaphoreType.DMA((2, 2, 2)),
                pltpu.SemaphoreType.DMA((2, 2, 2)),
                pltpu.SemaphoreType.DMA((1,)),
                pltpu.SemaphoreType.DMA((1,)),
                pltpu.SemaphoreType.DMA((1,)),
            ],
            compiler_params=pltpu.CompilerParams(
                collective_id=0, has_side_effects=True, vmem_limit_bytes=VMEM_BYTES
            ),
        )(slot_tile, tile_mask, token_count, queries, keys, values)
        return pl.pallas_call(
            settle,
            out_shape=jax.ShapeDtypeStruct((tok, width), jnp.bfloat16),
            in_specs=[pl.BlockSpec(memory_space=pl.ANY)],
            out_specs=pl.BlockSpec(memory_space=pl.ANY),
            scratch_shapes=[
                pltpu.VMEM((tok, width), jnp.bfloat16),
                pltpu.SemaphoreType.DMA((2, SETTLE_PARTS)),
            ],
            compiler_params=pltpu.CompilerParams(vmem_limit_bytes=VMEM_BYTES),
        )(attended)

    return jax.shard_map(
        shards,
        mesh=mesh,
        in_specs=(P(("tm", "tile"), None),) * 3 + (P(),) * 3,
        out_specs=P(("tm", "tile"), None),
        check_vma=False,
    )
```

```python
import functools

import jax
import jax.numpy as jnp
from jax import lax
from jax.experimental import pallas as pl
from jax.experimental.pallas import tpu as pltpu
from jax.sharding import PartitionSpec as P

HEAD_DIM = 128
KMAX = 11
SIDE = 4
RING = 8
OWNERS = SIDE * RING
SETTLE_PARTS = 4
VMEM_BYTES = 56 * 1024 * 1024
EXP2_SCALE = 1.4426950408889634 / HEAD_DIM**0.5
MESH = pl.DeviceIdType.MESH


def kernel(
    slabs,
    tiles,
    slot_hbm,
    mask_hbm,
    count_hbm,
    q_hbm,
    k_hbm,
    v_hbm,
    out_hbm,
    keys,
    values,
    query,
    result,
    live,
    score0,
    score1,
    top0,
    top1,
    k_raw,
    v_raw,
    k_fixed,
    v_fixed,
    slot_ref,
    mask_ref,
    count_ref,
    follow,
    block_of,
    key_pick,
    value_pick,
    plan_sem,
    send_sem,
    recv_sem,
    query_sem,
    own_sem,
    pass_sem,
    near_sem,
    out_send,
    out_recv,
    out_own,
):
    half_slabs = slabs // 2
    near = 3 * tiles
    slab = lax.axis_index("tm")
    slot = lax.axis_index("tile")
    half, place = slab // half_slabs, slab % half_slabs
    z, x = 2 * (slot // SIDE) + half, slot % SIDE
    tok = q_hbm.shape[0]

    def device(other_z, other_x):
        other_slab = (other_z % 2) * half_slabs + place
        return {"tm": other_slab, "tile": (other_z // 2) * SIDE + other_x}

    def partner(step):
        return (z + step + 1) % RING, (x + step // RING + 1) % SIDE

    def origin(step):
        return (z + 5 * RING - 1 - step) % RING, (x + 2 * SIDE - 1 - step // RING) % SIDE

    def block_at(other_z, other_x):
        return (other_z % 2) * tiles + (other_z // 2) * SIDE + other_x

    def head_columns(other_z, other_x):
        return pl.ds(pl.multiple_of((other_z * SIDE + other_x) * HEAD_DIM, HEAD_DIM), HEAD_DIM)

    upper, lower = pl.ds(0, tok // 2), pl.ds(tok // 2, tok // 2)
    first = [
        pltpu.make_async_copy(slot_hbm, slot_ref, plan_sem.at[0]),
        pltpu.make_async_copy(count_hbm, count_ref, plan_sem.at[1]),
        pltpu.make_async_copy(k_hbm.at[upper], k_raw.at[upper], plan_sem.at[2]),
        pltpu.make_async_copy(k_hbm.at[lower], k_raw.at[lower], plan_sem.at[3]),
        pltpu.make_async_copy(v_hbm, v_raw, plan_sem.at[4]),
        pltpu.make_async_copy(mask_hbm.at[place], mask_ref.at[0], plan_sem.at[5]),
        pltpu.make_async_copy(mask_hbm.at[place + half_slabs], mask_ref.at[1], plan_sem.at[6]),
    ]
    def beside(way):
        return {"tm": half * half_slabs + (place + half_slabs + way) % half_slabs}

    barrier = pltpu.get_barrier_semaphore()
    for reach in (4, 3, 5, 2, 6, 1, 7, 0):
        for shift in range(SIDE):
            if reach or shift:
                other = (z + reach) % RING, (x + shift) % SIDE
                pl.semaphore_signal(
                    barrier, inc=1, device_id=device(*other), device_id_type=MESH
                )
    for way in (1, -1):
        pl.semaphore_signal(barrier, inc=1, device_id=beside(way), device_id_type=MESH)
    for copy in first:
        copy.start()
    pl.semaphore_wait(barrier, OWNERS + 1)

    for copy in first[:4]:
        copy.wait()
    row = lax.broadcasted_iota(jnp.int32, (tok, HEAD_DIM), 0)
    own_count = count_ref[slab, slot_ref[slab, slot]]
    own_alive = jnp.where(row < own_count, 1.0, 0.0).astype(jnp.bfloat16)
    own_block = half * near + tiles + slot

    def k_block(columns):
        block = k_raw[:, columns]
        return block * own_alive + block[0:1] * (1 - own_alive)

    def v_block(columns):
        return v_raw[:, columns] * own_alive

    def own_query():
        return pltpu.make_async_copy(
            q_hbm.at[:, head_columns(z, x)], query.at[block_at(z, x)], own_sem.at[0]
        )

    spans = ((0, OWNERS // 2), (OWNERS // 2, OWNERS - 1))

    def spread(part):
        kind = part // 2
        start, stop = spans[part % 2]

        def send(step, carry):
            other = partner(step)
            columns = head_columns(*other)
            if kind == 0:
                k_fixed[step] = k_block(columns)
                source, target, arrived = k_fixed.at[step], keys.at[own_block], recv_sem.at[part]
            elif kind == 1:
                v_fixed[step] = v_block(columns)
                source, target, arrived = v_fixed.at[step], values.at[own_block], recv_sem.at[part]
            else:
                source, target = q_hbm.at[:, columns], query.at[block_at(z, x)]
                arrived = query_sem.at[block_at(z, x)]
            pltpu.make_async_remote_copy(
                src_ref=source,
                dst_ref=target,
                send_sem=send_sem.at[part],
                recv_sem=arrived,
                device_id=device(*other),
                device_id_type=MESH,
            ).start()
            return carry

        if part == 0:
            for step in range(start, stop):
                send(step, 0)
        else:
            lax.fori_loop(start, stop, send, 0)
        if part == 1:
            keys[own_block] = k_block(head_columns(z, x))
        elif part == 3:
            values[own_block] = v_block(head_columns(z, x))
        elif part == 5:
            own_query().start()

    def arrive(part):
        start, stop = spans[part % 2]
        blocks = (keys, values)[part // 2].at[pl.ds(0, stop - start)]
        pltpu.make_async_copy(blocks, blocks, recv_sem.at[part]).wait()

    def passing(kind, way, which):
        gathered = (keys, values)[kind]
        turned = place == (half_slabs - 1 if way > 0 else 0)
        target = which + way * turned.astype(jnp.int32)
        exists = (target >= 0) & (target < 2)
        target = jnp.clip(target, 0, 1)
        copy = pltpu.make_async_remote_copy(
            src_ref=gathered.at[pl.ds(which * near + tiles, tiles)],
            dst_ref=gathered.at[pl.ds(target * near + (0 if way > 0 else 2 * tiles), tiles)],
            send_sem=pass_sem.at[kind, (1 + way) // 2, which],
            recv_sem=near_sem.at[kind, (1 + way) // 2, target],
            device_id=beside(way),
            device_id_type=MESH,
        )
        return exists, copy

    def hand_on(kind):
        for way in (1, -1):
            for which in range(2):
                exists, copy = passing(kind, way, which)
                pl.when(exists)(copy.start)

    def handed_on(kind):
        for way in (1, -1):
            for which in range(2):
                exists, copy = passing(kind, way, which)
                pl.when(exists)(copy.wait_send)

    def near_arrive(kind):
        for way in (1, -1):
            for which in range(2):
                before = place + half_slabs * which - way
                blocks = (keys, values)[kind].at[pl.ds(0, tiles)]
                copy = pltpu.make_async_copy(
                    blocks, blocks, near_sem.at[kind, (1 + way) // 2, which]
                )
                pl.when((before >= 0) & (before < slabs))(copy.wait)

    spread(0)
    spread(1)
    for copy in first[4:]:
        copy.wait()

    nothing = jnp.zeros((tok, HEAD_DIM), jnp.bfloat16)
    live[2 * near] = nothing
    values[2 * near] = nothing
    for which in range(2):
        for block in range(3):
            there = jnp.clip(place + half_slabs * which + (block - 1), 0, slabs - 1)
            base = which * near + block * tiles

            def seat(index, carry, there=there, base=base):
                found = jnp.int32(0)
                for other in range(tiles):
                    found = jnp.where(slot_ref[there, other] == index, other, found)
                block_of[base + index] = base + found
                count = count_ref[there, slot_ref[there, index]]
                live[base + index] = jnp.where(row < count, 1.0, 0.0).astype(jnp.bfloat16)
                return carry

            lax.fori_loop(0, tiles, seat, 0)

        def chain(tile, carry, which=which):
            at = which * tiles + tile
            follow[at, near] = near
            follow[at, near + 1] = near

            def link(index, after):
                candidate = near - 1 - index
                listed = jnp.where(mask_ref[which, tile, candidate] > 0, candidate, after)
                follow[at, candidate] = listed
                return listed

            lax.fori_loop(0, near, link, jnp.int32(near))
            return carry

        lax.fori_loop(0, tiles, chain, 0)

        def pick(at, carry, which=which):
            tile = slot_ref[place + half_slabs * which, at]
            centre = block_of[which * near + tiles + tile]
            candidate = follow[which * tiles + tile, 0]
            for number in range(KMAX):
                listed = candidate < near
                spot = block_of[which * near + jnp.minimum(candidate, near - 1)]
                key_pick[which * tiles + at, number] = jnp.where(listed, spot, centre)
                value_pick[which * tiles + at, number] = jnp.where(listed, spot, 2 * near)
                candidate = follow[which * tiles + tile, candidate + 1]
            return carry

        lax.fori_loop(0, tiles, pick, 0)

    for part in range(4):
        arrive(part)
        if part % 2 == 1:
            hand_on(part // 2)
        spread(part + 2)

    def out_copy(step):
        other = origin(step)
        return pltpu.make_async_remote_copy(
            src_ref=result.at[block_at(*other)],
            dst_ref=out_hbm.at[:, head_columns(z, x)],
            send_sem=out_send.at[0],
            recv_sem=out_recv.at[0],
            device_id=device(*other),
            device_id_type=MESH,
        )

    def out_keep():
        return pltpu.make_async_copy(
            result.at[block_at(z, x)], out_hbm.at[:, head_columns(z, x)], out_own.at[0]
        )

    def work(ahead, ahead_scores, ahead_top, at=None, at_scores=None, at_top=None):
        q_tile = query[ahead]
        best = jnp.full((tok, HEAD_DIM), -jnp.inf, jnp.float32)
        if at is not None:
            top = jnp.concatenate([at_top[...]] * (tok // HEAD_DIM), axis=1)
            total = jnp.zeros((tok, 2 * HEAD_DIM), jnp.float32)
        for number in range(KMAX):
            score = lax.dot_general(
                q_tile,
                keys[key_pick[ahead, number]],
                (((1,), (1,)), ((), ())),
                preferred_element_type=jnp.float32,
            )
            ahead_scores[number] = score
            if at is not None:
                weight = jnp.exp2(at_scores[number] * EXP2_SCALE - top).astype(jnp.bfloat16)
                spot = value_pick[at, number]
                v_tile = jnp.concatenate([values[spot], live[spot]], axis=1)
                total = total + jnp.dot(weight, v_tile, preferred_element_type=jnp.float32)
            for start in range(0, tok, HEAD_DIM):
                best = jnp.maximum(best, score[:, start : start + HEAD_DIM])
        ahead_top[...] = jnp.broadcast_to(
            jnp.max(best, axis=1, keepdims=True) * EXP2_SCALE, (tok, HEAD_DIM)
        )
        if at is not None:
            attended = total[:, :HEAD_DIM] / total[:, HEAD_DIM:]
            at_half, at_slot = at // tiles, at % tiles
            at_slab = place + half_slabs * at_half
            count = count_ref[at_slab, slot_ref[at_slab, at_slot]]
            result[at] = jnp.where(row < count, attended, 0.0).astype(jnp.bfloat16)

    def query_arrive(step):
        at = block_at(*origin(step))

        @pl.when(step < OWNERS - 1)
        def _():
            block = query.at[at]
            pltpu.make_async_copy(block, block, query_sem.at[at]).wait()

        @pl.when(step == OWNERS - 1)
        def _():
            own_query().wait()

    near_arrive(0)
    near_arrive(1)
    query_arrive(0)
    work(block_at(*origin(0)), score0, top0)

    def turn(pair, carry):
        even = 2 * pair
        at, after = block_at(*origin(even)), block_at(*origin(even + 1))
        query_arrive(even + 1)
        work(after, score1, top1, at, score0, top0)
        out_copy(even).start()

        @pl.when(even + 2 < OWNERS)
        def _():
            query_arrive(even + 2)

        later = block_at(*origin(jnp.minimum(even + 2, OWNERS - 1)))
        work(later, score0, top0, after, score1, top1)

        @pl.when(even + 2 < OWNERS)
        def _():
            out_copy(even + 1).start()

        @pl.when(even + 2 == OWNERS)
        def _():
            out_keep().start()

        return carry

    lax.fori_loop(0, OWNERS // 2, turn, 0)

    blocks = out_hbm.at[:, pl.ds(0, (OWNERS - 1) * HEAD_DIM)]
    pltpu.make_async_copy(blocks, blocks, out_recv.at[0]).wait()
    out_keep().wait()
    gone = result.at[pl.ds(0, OWNERS - 1)]
    pltpu.make_async_copy(gone, gone, out_send.at[0]).wait()
    for part in range(6):
        start, stop = spans[part % 2]
        gone = query.at[pl.ds(0, stop - start)]
        pltpu.make_async_copy(gone, gone, send_sem.at[part]).wait()
    handed_on(0)
    handed_on(1)


def settle(source, target, held, sems):
    rows = source.shape[0] // SETTLE_PARTS
    spans = [pl.ds(part * rows, rows) for part in range(SETTLE_PARTS)]
    come = [pltpu.make_async_copy(source.at[s], held.at[s], sems.at[0, i]) for i, s in enumerate(spans)]
    go = [pltpu.make_async_copy(held.at[s], target.at[s], sems.at[1, i]) for i, s in enumerate(spans)]
    for copy in come:
        copy.start()
    for before, after in zip(come, go):
        before.wait()
        after.start()
    for copy in go:
        copy.wait()


def solution(mesh):
    slabs, tiles = mesh.shape["tm"], mesh.shape["tile"]

    def shards(queries, keys, values, slot_tile, tile_mask, token_count):
        tok, width = queries.shape
        near = 3 * tiles

        def blocks(number):
            return pltpu.VMEM((number, tok, HEAD_DIM), jnp.bfloat16)

        attended = pl.pallas_call(
            functools.partial(kernel, slabs, tiles),
            out_shape=jax.ShapeDtypeStruct((tok, width), jnp.bfloat16),
            in_specs=[pl.BlockSpec(memory_space=pl.ANY)] * 6,
            out_specs=pl.BlockSpec(memory_space=pl.ANY),
            scratch_shapes=[
                blocks(2 * near),
                blocks(2 * near + 1),
                blocks(2 * tiles),
                blocks(2 * tiles),
                blocks(2 * near + 1),
                pltpu.VMEM((KMAX, tok, tok), jnp.float32),
                pltpu.VMEM((KMAX, tok, tok), jnp.float32),
                pltpu.VMEM((tok, HEAD_DIM), jnp.float32),
                pltpu.VMEM((tok, HEAD_DIM), jnp.float32),
                pltpu.VMEM((tok, width), jnp.bfloat16),
                pltpu.VMEM((tok, width), jnp.bfloat16),
                blocks(OWNERS),
                blocks(OWNERS),
                pltpu.SMEM(slot_tile.shape, jnp.int32),
                pltpu.SMEM((2,) + tile_mask.shape[1:], jnp.int32),
                pltpu.SMEM(token_count.shape, jnp.int32),
                pltpu.SMEM((2 * tiles, near + 2), jnp.int32),
                pltpu.SMEM((2 * near,), jnp.int32),
                pltpu.SMEM((2 * tiles, KMAX), jnp.int32),
                pltpu.SMEM((2 * tiles, KMAX), jnp.int32),
                pltpu.SemaphoreType.DMA((7,)),
                pltpu.SemaphoreType.DMA((6,)),
                pltpu.SemaphoreType.DMA((4,)),
                pltpu.SemaphoreType.DMA((2 * tiles,)),
                pltpu.SemaphoreType.DMA((1,)),
                pltpu.SemaphoreType.DMA((2, 2, 2)),
                pltpu.SemaphoreType.DMA((2, 2, 2)),
                pltpu.SemaphoreType.DMA((1,)),
                pltpu.SemaphoreType.DMA((1,)),
                pltpu.SemaphoreType.DMA((1,)),
            ],
            compiler_params=pltpu.CompilerParams(
                collective_id=0, has_side_effects=True, vmem_limit_bytes=VMEM_BYTES
            ),
        )(slot_tile, tile_mask, token_count, queries, keys, values)
        return pl.pallas_call(
            settle,
            out_shape=jax.ShapeDtypeStruct((tok, width), jnp.bfloat16),
            in_specs=[pl.BlockSpec(memory_space=pl.ANY)],
            out_specs=pl.BlockSpec(memory_space=pl.ANY),
            scratch_shapes=[
                pltpu.VMEM((tok, width), jnp.bfloat16),
                pltpu.SemaphoreType.DMA((2, SETTLE_PARTS)),
            ],
            compiler_params=pltpu.CompilerParams(vmem_limit_bytes=VMEM_BYTES),
        )(attended)

    return jax.shard_map(
        shards,
        mesh=mesh,
        in_specs=(P(("tm", "tile"), None),) * 3 + (P(),) * 3,
        out_specs=P(("tm", "tile"), None),
        check_vma=False,
    )
```
